256 devices in a mesh: dp: 16 (over z_hi, x), seq: 16 (over z_lo, y, core).
Axes of the slice: x: 4, y: 4, z: 8 (z_hi: 4, z_lo: 2; z = z_hi * 2 + z_lo), core: 2. Of those that a mesh axis runs over, the one named last changes fastest.
Arguments:
- patches: bfloat16 [16, 4096, 1280], P('dp', 'seq'), may hold values from -72 to 72
- image_ids: int32 [16, 4096], P('dp'), may hold values from 0 to 3, never falling along the last dimension, each value on 1 to 2048 neighbouring positions
- w_qkv: bfloat16 [3, 1280, 1280], P(None, 'dp', 'seq'), may hold values from -0.15625 to 0.15625
- w_out: bfloat16 [1280, 1280], P('seq', 'dp'), may hold values from -0.3125 to 0.3125
Outputs:
- attended: bfloat16 [16, 4096, 1280], P('dp', 'seq')
The draws below stay inside these ranges and needn't reach their ends.
Inputs may be any that keep to these rules, and one draw needn't show every extreme that they name: `image_ids`: image numbers never fall along a row; each image has 1 to 2048 patches, one of them exactly that many.
All inputs are finite; a program needn't handle non-finite values.
Results may differ from the reference program's by a relative error of at most 0.0055.
The reference program's roundings to bfloat16 on the way (of `proj`, `probs` and `heads_out`) count: a program that leaves them out, or rounds other values in their place, can miss the bound.
Values may be sent and summed in bfloat16 or wider, within the bound.
A program may use at most 64 MiB of HBM per device.

```python
import math
import jax
import jax.numpy as jnp
import numpy as np
from jax import lax

D = 1280
HD = 80
SEQLEN = 4096
N_DP = 16


def draw_patches(key, part):
    key = jax.random.fold_in(key, 11)
    values = jnp.clip(2.0 * jax.random.normal(key, (N_DP, SEQLEN, D), jnp.float32), -12.0, 12.0)
    return values.astype(jnp.bfloat16)


def level_of(rng, shape, shards, low, largest):
    factor_of, own = 1.0, jax.random.fold_in(rng, 6)
    for position, parts in shards:
        draws = jnp.exp(jax.random.uniform(jax.random.fold_in(own, position), (parts,), jnp.float32, low / len(shards), largest / len(shards)))
        factor_of = factor_of * jnp.repeat(draws, shape[position] // parts).reshape([-1 if axis == position else 1 for axis in range(len(shape))])
    return factor_of


def length_profile(count, total, reach, lean):
    portions = [(1 << 20) // math.isqrt(rank ** lean) + 1 for rank in range(2, count + 1)]
    rest, counts = total - reach - (count - 1), [1] * (count - 1)
    while rest > 0:
        free = [i for i in range(count - 1) if counts[i] < reach]
        whole, budget = sum([portions[i] for i in free]), rest
        for i in free:
            addition = min(reach - counts[i], max(1, budget * portions[i] // whole), rest)
            counts[i] = counts[i] + addition
            rest = rest - addition
    return np.array([reach] + counts)


def ragged(stream_key, number_of, total, bound, skew):
    if number_of == 2:
        one = jax.random.randint(stream_key, (), max(1, total - bound), min(bound, total - 1) + 1)
        return jnp.stack([one, total - one])
    lengths = jnp.asarray(length_profile(number_of, total, bound, skew), jnp.int32)
    pairs = (number_of - 1) // 2
    source_of, receiver = lengths[1:1 + 2 * pairs:2], lengths[2:2 + 2 * pairs:2]
    margin = jnp.minimum(source_of - 1, bound - receiver)
    shifted = jax.random.randint(jax.random.fold_in(stream_key, 1), (pairs,), 0, 1 << 20) % (margin + 1)
    lengths = lengths.at[1:1 + 2 * pairs:2].set(source_of - shifted).at[2:2 + 2 * pairs:2].set(receiver + shifted)
    return lengths[jax.random.permutation(jax.random.fold_in(stream_key, 2), number_of)]


def centred(key, dims, deviation, bound, pieces=(), kind=jnp.bfloat16):
    entries = jax.random.normal(key, dims, jnp.float32) * deviation
    if len(pieces) > 0:
        entries = level_of(key, dims, pieces, -0.22, 0.18) * entries
    return jnp.clip(entries, min=-bound, max=bound).astype(kind)


def setup_inputs(seed: int = 0) -> dict:
    key_of = jax.random.split(jax.random.key(seed), 5)
    return {
        "patches": draw_patches(jax.random.fold_in(key_of[4], 71), 0),
        "image_ids": jax.vmap(lambda own: jnp.searchsorted(jnp.cumsum(ragged(own, 4, SEQLEN, SEQLEN // 2, 2)), jnp.arange(SEQLEN), side="right"))(jax.random.split(key_of[1], N_DP)).reshape((N_DP, SEQLEN)).astype(jnp.int32),
        "w_qkv": centred(key_of[2], (3, D, D), D ** -0.5, 0.15625, ((1, 16), (2, 16))),
        "w_out": centred(key_of[3], (D, D), (D // 4) ** -0.5, 0.3125, ((0, 16), (1, 16))),
    }


def attend(query, keys, values, ids):
    total = query.shape[0]
    width = query.shape[1]
    nheads = width // HD
    block = min(512, total)
    qh = query.reshape(total, nheads, HD).astype(jnp.float32)
    kh = keys.reshape(total, nheads, HD).astype(jnp.float32)
    vh = values.reshape(total, nheads, HD).astype(jnp.float32)

    def one_block(index):
        start = (index * block).astype(jnp.int32)
        qblock = lax.dynamic_slice_in_dim(qh, start, block, 0)
        idblock = lax.dynamic_slice_in_dim(ids, start, block, 0)
        scores = jnp.einsum('qhd,khd->hqk', qblock, kh) / jnp.sqrt(jnp.float32(HD))
        same = idblock[:, None] == ids[None, :]
        scores = jnp.where(same[None], scores, jnp.float32(-1e+30))
        top = lax.optimization_barrier(jnp.max(scores, axis=-1, keepdims=True))
        expd = jnp.exp(scores - top)
        probs = (expd / lax.optimization_barrier(jnp.sum(expd, axis=-1, keepdims=True))).astype(jnp.bfloat16)
        outs = jnp.einsum('hqk,khd->qhd', probs.astype(jnp.float32), vh)
        return outs.astype(jnp.bfloat16).reshape(block, width)
    blocks = lax.map(one_block, jnp.arange(total // block, dtype=jnp.int32))
    return blocks.reshape(total, width)

def reference(patches, image_ids, w_qkv, w_out):

    def one_row(args):
        row, ids = args
        proj = jnp.einsum('sd,tdc->tsc', row.astype(jnp.float32), w_qkv.astype(jnp.float32)).astype(jnp.bfloat16)
        heads_out = attend(proj[0], proj[1], proj[2], ids)
        return jnp.dot(heads_out, w_out, preferred_element_type=jnp.float32).astype(jnp.bfloat16)
    return lax.map(one_row, (patches, image_ids))
```

```python
import functools
import math

import jax
import jax.numpy as jnp
from jax import lax
from jax.experimental import pallas as pl
from jax.experimental.pallas import tpu as pltpu
from jax.sharding import PartitionSpec as P

MESH = pl.DeviceIdType.MESH
HD = 80
D = 1280
ROWS = 256
SEQ = 4096
PACK = 256
BF16 = jnp.bfloat16
F32 = jnp.float32


def place():
    dp, sq = lax.axis_index("dp"), lax.axis_index("seq")
    x = lax.rem(dp, 4)
    y = lax.rem(lax.div(sq, 2), 4)
    z = lax.div(dp, 4) * 2 + lax.div(sq, 8)
    return x, y, z, lax.rem(sq, 2)


def device(x, y, z, c):
    return (lax.div(z, 2) * 4 + x, lax.rem(z, 2) * 8 + y * 2 + c)


def project_kernel(x_ref, w_ref, qkv_ref, xbuf, wbuf, pbuf, ssem, rsem, lsem):
    x, y, z, c = place()
    zl = lax.rem(z, 2)
    xp, xm, x2 = lax.rem(x + 1, 4), lax.rem(x + 3, 4), lax.rem(x + 2, 4)
    yp, ym, y2 = lax.rem(y + 1, 4), lax.rem(y + 3, 4), lax.rem(y + 2, 4)
    zp, zm = lax.rem(z + 1, 8), lax.rem(z + 7, 8)
    co = 1 - c
    mate = z + 1 - 2 * zl
    to_xp, to_xm = device(xp, y, z, c), device(xm, y, z, c)
    to_yp, to_ym = device(x, yp, z, c), device(x, ym, z, c)
    to_zp, to_zm = device(x, y, zp, c), device(x, y, zm, c)
    to_co, to_mate = device(x, y, z, co), device(x, y, mate, c)

    barrier = pltpu.get_barrier_semaphore()
    for to in (to_xp, to_xm, to_yp, to_ym, to_zp, to_zm, to_co):
        pl.semaphore_signal(barrier, inc=1, device_id=to, device_id_type=MESH)
    pl.semaphore_wait(barrier, 7)

    sent = []

    def copy(src, dst, k, to):
        return pltpu.make_async_remote_copy(
            src_ref=src,
            dst_ref=dst,
            send_sem=ssem.at[k],
            recv_sem=rsem.at[k],
            device_id=to,
            device_id_type=MESH,
        )

    def send(src, dst, k, to):
        cp = copy(src, dst, k, to)
        cp.start()
        sent.append(cp)

    def arrived(dst, k):
        copy(dst, dst, k, to_co).wait_recv()

    def wslot(zz, xx):
        row = pl.multiple_of((lax.div(zz, 2) * 4 + xx) * HD, 16)
        return wbuf.at[lax.rem(zz, 2), pl.ds(row, HD), :]

    def zslot(j):
        return lax.rem(z + 8 - j, 8) if j <= 4 else lax.rem(z + j - 4, 8)

    def xid(j, k):
        return 7 + 3 * j + k

    half = ROWS // 2

    def xpart(cc, yy, part):
        return xbuf.at[cc, yy, pl.ds(part * half, half), :]

    send(w_ref, wslot(z, x), 0, to_zp)
    send(w_ref, wslot(z, x), 4, to_zm)
    send(w_ref, wslot(z, x), xid(0, 0), to_xp)
    send(w_ref, wslot(z, x), xid(0, 1), to_xm)
    for part in (0, 1):
        src = x_ref.at[pl.ds(part * half, half), :]
        send(src, xpart(c, y, part), 31 + part, to_yp)
        src = x_ref.at[pl.ds((1 - part) * half, half), :]
        send(src, xpart(c, y, 1 - part), 34 - part, to_ym)
    send(x_ref, xbuf.at[c, y], 37, to_co)
    own_w = pltpu.make_async_copy(w_ref, wslot(z, x), lsem.at[8])
    own_w.start()
    own_x = pltpu.make_async_copy(x_ref, xbuf.at[c, y], lsem.at[9])
    own_x.start()

    def x_forward(j):
        zz = zslot(j)
        if j % 2 == 0:
            arrived(wslot(zz, xm), xid(j, 0))
            send(wslot(zz, xm), wslot(zz, xm), xid(j, 2), to_xp)
        else:
            arrived(wslot(zz, xp), xid(j, 1))
            send(wslot(zz, xp), wslot(zz, xp), xid(j, 2), to_xm)

    before = 0
    for j in (1, 5, 2, 6, 3, 7, 4):
        here = wslot(zslot(j), x)
        arrived(here, j - 1)
        if j in (1, 2, 3):
            send(here, here, j, to_zp)
        if j in (5, 6):
            send(here, here, j, to_zm)
        send(here, here, xid(j, 0), to_xp)
        send(here, here, xid(j, 1), to_xm)
        x_forward(before)
        before = j
    x_forward(before)

    arrived(xpart(c, ym, 0), 31)
    send(xpart(c, ym, 0), xpart(c, ym, 0), 35, to_yp)
    arrived(xpart(c, yp, 1), 34)
    send(xpart(c, yp, 1), xpart(c, yp, 1), 36, to_ym)

    for j in range(8):
        zz = zslot(j)
        if j % 2 == 0:
            arrived(wslot(zz, xp), xid(j, 1))
        else:
            arrived(wslot(zz, xm), xid(j, 0))
        arrived(wslot(zz, x2), xid(j, 2))
    own_w.wait()

    kept = []

    def block(cc, yy):
        source = zl * 8 + yy * 2 + cc
        return qkv_ref.at[pl.ds(pl.multiple_of(source * ROWS, ROWS), ROWS), :]

    def project(i, cc, yy):
        patches = xbuf[cc, yy]
        for whose, head in ((0, 1 - zl), (1, zl)):
            pbuf[i, whose] = jnp.dot(
                patches, wbuf[head], preferred_element_type=F32
            ).astype(BF16)
            if whose == 0:
                send(pbuf.at[i, 0], block(cc, yy), 41 + i, to_mate)
            else:
                keep = pltpu.make_async_copy(pbuf.at[i, 1], block(cc, yy), lsem.at[i])
                keep.start()
                kept.append(keep)

    own_x.wait()
    project(0, c, y)
    arrived(xbuf.at[co, y], 37)
    project(1, co, y)
    arrived(xpart(c, ym, 1), 32)
    send(xbuf.at[c, ym], xbuf.at[c, ym], 38, to_co)
    arrived(xpart(c, yp, 0), 33)
    send(xbuf.at[c, yp], xbuf.at[c, yp], 39, to_co)
    project(2, c, ym)
    project(3, c, yp)
    arrived(xbuf.at[co, ym], 38)
    project(4, co, ym)
    arrived(xbuf.at[co, yp], 39)
    project(5, co, yp)
    arrived(xpart(c, y2, 0), 35)
    arrived(xpart(c, y2, 1), 36)
    send(xbuf.at[c, y2], xbuf.at[c, y2], 40, to_co)
    project(6, c, y2)
    arrived(xbuf.at[co, y2], 40)
    project(7, co, y2)

    theirs = 1 - zl
    for i, (cc, yy) in enumerate(
        ((c, y), (co, y), (c, ym), (c, yp), (co, ym), (co, yp), (c, y2), (co, y2))
    ):
        source = theirs * 8 + yy * 2 + cc
        dst = qkv_ref.at[pl.ds(pl.multiple_of(source * ROWS, ROWS), ROWS), :]
        arrived(dst, 41 + i)
    for keep in kept:
        keep.wait()
    for cp in sent:
        cp.wait_send()


def project(patches, w):
    return pl.pallas_call(
        project_kernel,
        out_shape=jax.ShapeDtypeStruct((SEQ, PACK), BF16),
        in_specs=[
            pl.BlockSpec(memory_space=pl.ANY),
            pl.BlockSpec(memory_space=pltpu.VMEM),
        ],
        out_specs=pl.BlockSpec(memory_space=pl.ANY),
        scratch_shapes=[
            pltpu.VMEM((2, 4, ROWS, D), BF16),
            pltpu.VMEM((2, D, PACK), BF16),
            pltpu.VMEM((8, 2, ROWS, PACK), BF16),
            pltpu.SemaphoreType.DMA((49,)),
            pltpu.SemaphoreType.DMA((49,)),
            pltpu.SemaphoreType.DMA((10,)),
        ],
        compiler_params=pltpu.CompilerParams(
            collective_id=0, has_side_effects=True, vmem_limit_bytes=40 << 20
        ),
        name="project",
    )(patches, w)


TQ = 256
CK = 512
SCALE = math.log2(math.e) / math.sqrt(HD)


def fold(op, a):
    parts = [a[:, i : i + 128] for i in range(0, a.shape[1], 128)]
    while len(parts) > 1:
        parts = [op(parts[i], parts[i + 1]) for i in range(0, len(parts), 2)]
    return parts[0]


def attend_kernel(ids_ref, qkv_ref, o_ref, kaug, scores):
    ids = ids_ref[...]
    cuts = [
        jnp.sum((ids < a).astype(F32)).astype(jnp.int32) for a in (1, 2, 3)
    ]

    def image_of(start, rows):
        pos = lax.broadcasted_iota(jnp.int32, (rows, 128), 0) + start
        return sum((pos >= cut).astype(jnp.int32) for cut in cuts)

    lane = lax.broadcasted_iota(jnp.int32, (TQ, 128), 1)

    @pl.loop(0, SEQ // TQ)
    def _(i):
        rows = pl.ds(pl.multiple_of(i * TQ, TQ), TQ)
        keys = qkv_ref[rows, 128:256].astype(F32)
        other = jnp.where(image_of(i * TQ, TQ) != lane - HD, 1.0, 0.0)
        kaug[rows, :] = jnp.where(lane < HD, keys, other).astype(BF16)

    @pl.loop(0, SEQ // TQ)
    def _(i):
        first = i * TQ
        rows = pl.ds(pl.multiple_of(first, TQ), TQ)
        lo, hi = jnp.int32(0), jnp.int32(SEQ)
        for cut in cuts:
            lo = jnp.maximum(lo, jnp.where(cut <= first, cut, 0))
            hi = jnp.minimum(hi, jnp.where(cut >= first + TQ, cut, SEQ))
        j0, j1 = lax.div(lo, CK), lax.div(hi + CK - 1, CK)
        query = qkv_ref[rows, 0:128].astype(F32)
        own = jnp.where(image_of(first, TQ) == lane - HD, -1e30, 0.0)
        query = jnp.where(lane < HD, query, own).astype(BF16)

        def score(j, top):
            cols = pl.ds(pl.multiple_of(j * CK, CK), CK)
            s = lax.dot_general(
                query, kaug[cols, :], (((1,), (1,)), ((), ())),
                preferred_element_type=F32,
            )
            scores[:, cols] = s
            return jnp.maximum(top, fold(jnp.maximum, s))

        top = lax.fori_loop(j0, j1, score, jnp.full((TQ, 128), -jnp.inf, F32))
        top = jnp.max(top, axis=1, keepdims=True)

        def mix(j, carry):
            total, acc = carry
            cols = pl.ds(pl.multiple_of(j * CK, CK), CK)
            e = jnp.exp2((scores[:, cols] - top) * SCALE)
            total = total + fold(jnp.add, e)
            acc = acc + jnp.dot(
                e.astype(BF16), qkv_ref[cols, :], preferred_element_type=F32
            )
            return total, acc

        total, acc = lax.fori_loop(
            j0, j1, mix, (jnp.zeros((TQ, 128), F32), jnp.zeros((TQ, PACK), F32))
        )
        out = acc / jnp.sum(total, axis=1, keepdims=True)
        out = out.T.astype(BF16)
        o_ref[0:48, rows] = out[80:128]
        o_ref[48:80, rows] = out[208:240]


def attend(ids, qkv):
    return pl.pallas_call(
        attend_kernel,
        out_shape=jax.ShapeDtypeStruct((HD, SEQ), BF16),
        in_specs=[pl.BlockSpec(memory_space=pltpu.VMEM)] * 2,
        out_specs=pl.BlockSpec(memory_space=pltpu.VMEM),
        scratch_shapes=[
            pltpu.VMEM((SEQ, 128), BF16),
            pltpu.VMEM((TQ, SEQ), F32),
        ],
        compiler_params=pltpu.CompilerParams(vmem_limit_bytes=40 << 20),
        name="attend",
    )(ids, qkv)


def output_kernel(o_ref, wg_ref, out_ref, held, whole, ssem, rsem):
    dp, me = lax.axis_index("dp"), lax.axis_index("seq")
    barrier = pltpu.get_barrier_semaphore()
    for k in range(1, 16):
        to = (dp, lax.rem(me + k, 16))
        pl.semaphore_signal(barrier, inc=1, device_id=to, device_id_type=MESH)
    pl.semaphore_wait(barrier, 15)

    def mine(k):
        cols = pl.ds(pl.multiple_of(lax.rem(me + k, 16) * ROWS, ROWS), ROWS)
        return o_ref.at[:, cols]

    def slot(s):
        return held.at[pl.ds(pl.multiple_of(s * HD, 16), HD), :]

    copies = []
    for k in range(1, 16):
        cp = pltpu.make_async_remote_copy(
            src_ref=mine(k),
            dst_ref=slot(me),
            send_sem=ssem.at[k],
            recv_sem=rsem.at[k],
            device_id=(dp, lax.rem(me + k, 16)),
            device_id_type=MESH,
        )
        cp.start()
        copies.append(cp)
    own = pltpu.make_async_copy(mine(0), slot(me), ssem.at[0])
    own.start()
    for d in range(16):
        whole[:, d * HD : (d + 1) * HD] = wg_ref[d]
    own.wait()
    for k in range(1, 16):
        frm = slot(lax.rem(me + 16 - k, 16))
        pltpu.make_async_remote_copy(
            src_ref=frm,
            dst_ref=frm,
            send_sem=ssem.at[k],
            recv_sem=rsem.at[k],
            device_id=(dp, lax.rem(me + k, 16)),
            device_id_type=MESH,
        ).wait_recv()
    out_ref[...] = lax.dot_general(
        held[...], whole[...], (((0,), (0,)), ((), ())), preferred_element_type=F32
    ).astype(BF16)
    for cp in copies:
        cp.wait_send()


def output(o, wg):
    return pl.pallas_call(
        output_kernel,
        out_shape=jax.ShapeDtypeStruct((ROWS, D), BF16),
        in_specs=[pl.BlockSpec(memory_space=pltpu.VMEM)] * 2,
        out_specs=pl.BlockSpec(memory_space=pltpu.VMEM),
        scratch_shapes=[
            pltpu.VMEM((D, ROWS), BF16),
            pltpu.VMEM((D, D), BF16),
            pltpu.SemaphoreType.DMA((16,)),
            pltpu.SemaphoreType.DMA((16,)),
        ],
        compiler_params=pltpu.CompilerParams(
            collective_id=1, has_side_effects=True, vmem_limit_bytes=40 << 20
        ),
        name="output",
    )(o, wg)


def shards(patches, image_ids, w_qkv, w_out):
    q, k, v = w_qkv[0], w_qkv[1], w_qkv[2]
    spare = jnp.zeros((HD, PACK - 3 * HD), BF16)
    w = jnp.concatenate([q, v[:, :48], k, v[:, 48:], spare], axis=1)
    wg = lax.all_gather(w_out, ("dp", "seq"), axis=0, tiled=True)
    qkv = project(patches[0], w)
    o = attend(image_ids.reshape(SEQ // 128, 128), qkv)
    out = output(o, wg.reshape(16, D, HD))
    return out[None]


def solution(mesh):
    return jax.shard_map(
        shards,
        mesh=mesh,
        in_specs=(P("dp", "seq", None), P("dp", None), P(None, "dp", "seq"), P("seq", "dp")),
        out_specs=P("dp", "seq", None),
        check_vma=False,
    )
```

```python
import itertools
import math

import jax
import jax.numpy as jnp
from jax import lax
from jax.experimental import pallas as pl
from jax.experimental.pallas import tpu as pltpu
from jax.sharding import PartitionSpec as P

MESH = pl.DeviceIdType.MESH
HD = 80
D = 1280
ROWS = 256
SEQ = 4096
PACK = 256
BF16 = jnp.bfloat16
F32 = jnp.float32


def place():
    dp, sq = lax.axis_index("dp"), lax.axis_index("seq")
    x = lax.rem(dp, 4)
    y = lax.rem(lax.div(sq, 2), 4)
    z = lax.div(dp, 4) * 2 + lax.div(sq, 8)
    return x, y, z, lax.rem(sq, 2)


def device(x, y, z, c):
    return (lax.div(z, 2) * 4 + x, lax.rem(z, 2) * 8 + y * 2 + c)


def project_kernel(
    x_ref, w_ref, qkv_ref, wo_ref, xbuf, wbuf, pbuf, zbuf, pack, ssem, rsem, lsem
):
    x, y, z, c = place()
    zl = lax.rem(z, 2)
    xp, xm, x2 = lax.rem(x + 1, 4), lax.rem(x + 3, 4), lax.rem(x + 2, 4)
    yp, ym, y2 = lax.rem(y + 1, 4), lax.rem(y + 3, 4), lax.rem(y + 2, 4)
    co = 1 - c
    mate = z + 1 - 2 * zl
    to_x = [device(xx, y, z, c) for xx in (xp, xm, x2)]
    to_y = [device(x, yy, z, c) for yy in (yp, ym, y2)]
    to_z = {d: device(x, y, lax.rem(z + d, 8), c) for d in range(1, 8)}
    to_co, to_mate = device(x, y, z, co), device(x, y, mate, c)

    barrier = pltpu.get_barrier_semaphore()
    for to in (*to_x, *to_y, *to_z.values(), to_co):
        pl.semaphore_signal(barrier, inc=1, device_id=to, device_id_type=MESH)
    pl.semaphore_wait(barrier, 14)

    sent, names, local = [], {}, []

    def sem(*name):
        return names.setdefault(name, len(names))

    def copy(src, dst, k, to):
        return pltpu.make_async_remote_copy(
            src_ref=src,
            dst_ref=dst,
            send_sem=ssem.at[k],
            recv_sem=rsem.at[k],
            device_id=to,
            device_id_type=MESH,
        )

    def send(src, dst, to, *name):
        cp = copy(src, dst, sem(*name), to)
        cp.start()
        sent.append(cp)

    def arrived(dst, *name):
        copy(dst, dst, sem(*name), to_co).wait_recv()

    def keep(src, dst):
        cp = pltpu.make_async_copy(src, dst, lsem.at[len(local)])
        cp.start()
        local.append(cp)
        return cp

    def behind(d):
        return lax.rem(z + 8 - d, 8)

    def wslot(zz, xx):
        row = pl.multiple_of((lax.div(zz, 2) * 4 + xx) * HD, 16)
        return wbuf.at[lax.rem(zz, 2), pl.ds(row, HD), :]

    half = ROWS // 2

    def xpart(cc, yy, part):
        return xbuf.at[cc, yy, pl.ds(part * half, half), :]

    w_mine, wo_mine = w_ref.at[:, 0:PACK], w_ref.at[:, PACK : PACK + 128]
    for d in (1, 7, 3, 5, 2, 6, 4):
        send(w_mine, wslot(z, x), to_z[d], "wz", d)
    for to, k in zip(to_x, range(3)):
        send(w_mine, wslot(z, x), to, "wx", 0, k)
    for d in (1, 7, 2, 6, 3, 5, 4):
        send(wo_mine, zbuf.at[z], to_z[d], "oz", d)
    for part in (0, 1):
        src = x_ref.at[pl.ds(part * half, half), :]
        send(src, xpart(c, y, part), to_y[0], "y+", part)
        src = x_ref.at[pl.ds((1 - part) * half, half), :]
        send(src, xpart(c, y, 1 - part), to_y[1], "y-", 1 - part)
    send(x_ref, xbuf.at[c, y], to_co, "c", 0)
    own_x = keep(x_ref, xbuf.at[c, y])
    own_w = keep(w_mine, wslot(z, x))
    own_o = keep(wo_mine, zbuf.at[z])

    for d in (1, 7, 3, 5, 2, 6, 4):
        here = wslot(behind(d), x)
        arrived(here, "wz", d)
        for to, k in zip(to_x, range(3)):
            send(here, here, to, "wx", d, k)

    for d in range(1, 8):
        arrived(zbuf.at[behind(d)], "oz", d)
    own_o.wait()
    for zz in range(8):
        lane = (zz % 2) * 4 * HD + (zz // 2) * HD
        pack[:, lane : lane + HD] = zbuf[zz][:, :HD]
    for to, k in zip(to_y, range(3)):
        send(pack, wo_ref.at[c, x, y], to, "oy", k)
    own_pack = keep(pack, wo_ref.at[c, x, y])

    arrived(xpart(c, ym, 0), "y+", 0)
    send(xpart(c, ym, 0), xpart(c, ym, 0), to_y[0], "y2", 0)
    arrived(xpart(c, yp, 1), "y-", 1)
    send(xpart(c, yp, 1), xpart(c, yp, 1), to_y[1], "y2", 1)

    def w_here(ds):
        for d in ds:
            for k, xx in enumerate((xm, xp, x2)):
                arrived(wslot(behind(d), xx), "wx", d, k)

    def block(lo, cc, yy):
        row = pl.multiple_of((lo * 8 + yy * 2 + cc) * ROWS, ROWS)
        return qkv_ref.at[pl.ds(row, ROWS), :]

    places = ((c, y), (co, y), (c, ym), (c, yp), (co, ym), (co, yp), (c, y2), (co, y2))

    def project(i, whose):
        head = zl if whose else 1 - zl
        cc, yy = places[i]
        pbuf[i, whose] = jnp.dot(
            xbuf[cc, yy], wbuf[head], preferred_element_type=F32
        ).astype(BF16)
        if whose:
            keep(pbuf.at[i, 1], block(zl, cc, yy))
        else:
            send(pbuf.at[i, 0], block(zl, cc, yy), to_mate, "mate", i)

    w_here((1, 7, 3, 5))
    own_x.wait()
    project(0, 0)
    arrived(xbuf.at[co, y], "c", 0)
    project(1, 0)
    own_w.wait()
    w_here((0, 2, 6, 4))
    project(0, 1)
    project(1, 1)

    own_pack.wait()
    for k, yy in enumerate((y, ym, yp, y2)):
        here = wo_ref.at[c, x, yy]
        if k:
            arrived(here, "oy", k - 1)
        send(here, here, to_x[0], "ox", k, 0)
        send(here, here, to_x[1], "ox", k, 1)

    arrived(xpart(c, ym, 1), "y+", 1)
    send(xbuf.at[c, ym], xbuf.at[c, ym], to_co, "c", 1)
    arrived(xpart(c, yp, 0), "y-", 0)
    send(xbuf.at[c, yp], xbuf.at[c, yp], to_co, "c", 2)
    project(2, 0)
    project(3, 0)
    arrived(xbuf.at[co, ym], "c", 1)
    project(4, 0)
    arrived(xbuf.at[co, yp], "c", 2)
    project(5, 0)
    for i in (2, 3, 4, 5):
        project(i, 1)

    for k, yy in enumerate((y, ym, yp, y2)):
        side = k % 2
        here = wo_ref.at[c, (xm, xp)[side], yy]
        arrived(here, "ox", k, side)
        send(here, here, to_x[side], "ox", k, 2)

    arrived(xpart(c, y2, 0), "y2", 0)
    arrived(xpart(c, y2, 1), "y2", 1)
    send(xbuf.at[c, y2], xbuf.at[c, y2], to_co, "c", 3)
    project(6, 0)
    arrived(xbuf.at[co, y2], "c", 3)
    project(7, 0)
    project(6, 1)
    project(7, 1)

    send(wo_ref.at[c, x], wo_ref.at[c, x], to_co, "oc", 0)
    for k, yy in enumerate((y, ym, yp, y2)):
        side = 1 - k % 2
        arrived(wo_ref.at[c, (xm, xp)[side], yy], "ox", k, side)
    send(wo_ref.at[c, xm], wo_ref.at[c, xm], to_co, "oc", 1)
    send(wo_ref.at[c, xp], wo_ref.at[c, xp], to_co, "oc", 2)
    for k, yy in enumerate((y, ym, yp, y2)):
        arrived(wo_ref.at[c, x2, yy], "ox", k, 2)
    send(wo_ref.at[c, x2], wo_ref.at[c, x2], to_co, "oc", 3)
    for i, (cc, yy) in enumerate(places):
        arrived(block(1 - zl, cc, yy), "mate", i)
    for k, xx in enumerate((x, xm, xp, x2)):
        arrived(wo_ref.at[co, xx], "oc", k)
    for cp in local[4:]:
        cp.wait()
    for cp in sent:
        cp.wait_send()


def project(patches, w):
    return pl.pallas_call(
        project_kernel,
        out_shape=(
            jax.ShapeDtypeStruct((SEQ, PACK), BF16),
            jax.ShapeDtypeStruct((2, 4, 4, HD, 8 * HD), BF16),
        ),
        in_specs=[
            pl.BlockSpec(memory_space=pl.ANY),
            pl.BlockSpec(memory_space=pltpu.VMEM),
        ],
        out_specs=(pl.BlockSpec(memory_space=pl.ANY),) * 2,
        scratch_shapes=[
            pltpu.VMEM((2, 4, ROWS, D), BF16),
            pltpu.VMEM((2, D, PACK), BF16),
            pltpu.VMEM((8, 2, ROWS, PACK), BF16),
            pltpu.VMEM((8, HD, 128), BF16),
            pltpu.VMEM((HD, 8 * HD), BF16),
            pltpu.SemaphoreType.DMA((80,)),
            pltpu.SemaphoreType.DMA((80,)),
            pltpu.SemaphoreType.DMA((16,)),
        ],
        compiler_params=pltpu.CompilerParams(
            collective_id=0, has_side_effects=True, vmem_limit_bytes=40 << 20
        ),
        name="project",
    )(patches, w)


TQ = 256
CK = 512
SCALE = math.log2(math.e) / math.sqrt(HD)


def fold(op, a):
    parts = [a[:, i : i + 128] for i in range(0, a.shape[1], 128)]
    while len(parts) > 1:
        parts = [op(parts[i], parts[i + 1]) for i in range(0, len(parts), 2)]
    return parts[0]


def attend_kernel(ids_ref, qkv_ref, o_ref, kaug, scores):
    ids = ids_ref[...]
    cuts = [
        jnp.sum((ids < a).astype(F32)).astype(jnp.int32) for a in (1, 2, 3)
    ]

    def image_of(start, rows):
        pos = lax.broadcasted_iota(jnp.int32, (rows, 128), 0) + start
        return sum((pos >= cut).astype(jnp.int32) for cut in cuts)

    lane = lax.broadcasted_iota(jnp.int32, (TQ, 128), 1)

    @pl.loop(0, SEQ // TQ)
    def _(i):
        rows = pl.ds(pl.multiple_of(i * TQ, TQ), TQ)
        keys = qkv_ref[rows, 128:256].astype(F32)
        other = jnp.where(image_of(i * TQ, TQ) != lane - HD, 1.0, 0.0)
        kaug[rows, :] = jnp.where(lane < HD, keys, other).astype(BF16)

    @pl.loop(0, SEQ // TQ)
    def _(i):
        first = i * TQ
        rows = pl.ds(pl.multiple_of(first, TQ), TQ)
        lo, hi = jnp.int32(0), jnp.int32(SEQ)
        for cut in cuts:
            lo = jnp.maximum(lo, jnp.where(cut <= first, cut, 0))
            hi = jnp.minimum(hi, jnp.where(cut >= first + TQ, cut, SEQ))
        j0, j1 = lax.div(lo, CK), lax.div(hi + CK - 1, CK)
        query = qkv_ref[rows, 0:128].astype(F32)
        own = jnp.where(image_of(first, TQ) == lane - HD, -1e30, 0.0)
        query = jnp.where(lane < HD, query, own).astype(BF16)

        def score(j, top):
            cols = pl.ds(pl.multiple_of(j * CK, CK), CK)
            s = lax.dot_general(
                query, kaug[cols, :], (((1,), (1,)), ((), ())),
                preferred_element_type=F32,
            )
            scores[:, cols] = s
            return jnp.maximum(top, fold(jnp.maximum, s))

        top = lax.fori_loop(j0, j1, score, jnp.full((TQ, 128), -jnp.inf, F32))
        top = jnp.max(top, axis=1, keepdims=True)

        def mix(j, carry):
            total, acc = carry
            cols = pl.ds(pl.multiple_of(j * CK, CK), CK)
            e = jnp.exp2((scores[:, cols] - top) * SCALE)
            total = total + fold(jnp.add, e)
            acc = acc + jnp.dot(
                e.astype(BF16), qkv_ref[cols, :], preferred_element_type=F32
            )
            return total, acc

        total, acc = lax.fori_loop(
            j0, j1, mix, (jnp.zeros((TQ, 128), F32), jnp.zeros((TQ, PACK), F32))
        )
        out = acc / jnp.sum(total, axis=1, keepdims=True)
        out = out.T.astype(BF16)
        o_ref[0:48, rows] = out[80:128]
        o_ref[48:80, rows] = out[208:240]


def attend(ids, qkv):
    return pl.pallas_call(
        attend_kernel,
        out_shape=jax.ShapeDtypeStruct((HD, SEQ), BF16),
        in_specs=[pl.BlockSpec(memory_space=pltpu.VMEM)] * 2,
        out_specs=pl.BlockSpec(memory_space=pltpu.VMEM),
        scratch_shapes=[
            pltpu.VMEM((SEQ, 128), BF16),
            pltpu.VMEM((TQ, SEQ), F32),
        ],
        compiler_params=pltpu.CompilerParams(vmem_limit_bytes=40 << 20),
        name="attend",
    )(ids, qkv)


def output_kernel(o_ref, wg_ref, out_ref, held, whole, ssem, rsem):
    dp, me = lax.axis_index("dp"), lax.axis_index("seq")
    barrier = pltpu.get_barrier_semaphore()
    for k in range(1, 16):
        to = (dp, lax.rem(me + k, 16))
        pl.semaphore_signal(barrier, inc=1, device_id=to, device_id_type=MESH)
    pl.semaphore_wait(barrier, 15)

    def mine(k):
        cols = pl.ds(pl.multiple_of(lax.rem(me + k, 16) * ROWS, ROWS), ROWS)
        return o_ref.at[:, cols]

    def slot(s):
        return held.at[pl.ds(pl.multiple_of(s * HD, 16), HD), :]

    copies = []
    for k in range(1, 16):
        cp = pltpu.make_async_remote_copy(
            src_ref=mine(k),
            dst_ref=slot(me),
            send_sem=ssem.at[k],
            recv_sem=rsem.at[k],
            device_id=(dp, lax.rem(me + k, 16)),
            device_id_type=MESH,
        )
        cp.start()
        copies.append(cp)
    own = pltpu.make_async_copy(mine(0), slot(me), ssem.at[0])
    own.start()

    @pl.loop(0, 8)
    def _(i):
        for zl, x, zh in itertools.product(range(2), range(4), range(4)):
            row = pl.multiple_of((zl * 8 + i) * HD, 16)
            col, lane = (zh * 4 + x) * HD, (zl * 4 + zh) * HD
            whole[pl.ds(row, HD), col : col + HD] = wg_ref[
                lax.rem(i, 2), x, lax.div(i, 2), :, lane : lane + HD
            ]

    own.wait()
    for k in range(1, 16):
        frm = slot(lax.rem(me + 16 - k, 16))
        pltpu.make_async_remote_copy(
            src_ref=frm,
            dst_ref=frm,
            send_sem=ssem.at[k],
            recv_sem=rsem.at[k],
            device_id=(dp, lax.rem(me + k, 16)),
            device_id_type=MESH,
        ).wait_recv()
    out_ref[...] = lax.dot_general(
        held[...], whole[...], (((0,), (0,)), ((), ())), preferred_element_type=F32
    ).astype(BF16)
    for cp in copies:
        cp.wait_send()


def output(o, wg):
    return pl.pallas_call(
        output_kernel,
        out_shape=jax.ShapeDtypeStruct((ROWS, D), BF16),
        in_specs=[pl.BlockSpec(memory_space=pltpu.VMEM)] * 2,
        out_specs=pl.BlockSpec(memory_space=pltpu.VMEM),
        scratch_shapes=[
            pltpu.VMEM((D, ROWS), BF16),
            pltpu.VMEM((D, D), BF16),
            pltpu.SemaphoreType.DMA((16,)),
            pltpu.SemaphoreType.DMA((16,)),
        ],
        compiler_params=pltpu.CompilerParams(
            collective_id=1, has_side_effects=True, vmem_limit_bytes=40 << 20
        ),
        name="output",
    )(o, wg)


def shards(patches, image_ids, w_qkv, w_out):
    q, k, v = w_qkv[0], w_qkv[1], w_qkv[2]
    spare = jnp.zeros((HD, PACK - 3 * HD), BF16)
    more = jnp.zeros((HD, 128 - HD), BF16)
    w = jnp.concatenate([q, v[:, :48], k, v[:, 48:], spare, w_out, more], axis=1)
    qkv, wo = project(patches[0], w)
    o = attend(image_ids.reshape(SEQ // 128, 128), qkv)
    out = output(o, wo)
    return out[None]


def solution(mesh):
    return jax.shard_map(
        shards,
        mesh=mesh,
        in_specs=(P("dp", "seq", None), P("dp", None), P(None, "dp", "seq"), P("seq", "dp")),
        out_specs=P("dp", "seq", None),
        check_vma=False,
    )
```

```python
import functools
import itertools
import math

import jax
import jax.numpy as jnp
from jax import lax
from jax.experimental import pallas as pl
from jax.experimental.pallas import tpu as pltpu
from jax.sharding import PartitionSpec as P

MESH = pl.DeviceIdType.MESH
HD = 80
D = 1280
ROWS = 256
SEQ = 4096
PACK = 256
BF16 = jnp.bfloat16
F32 = jnp.float32


def place():
    dp, sq = lax.axis_index("dp"), lax.axis_index("seq")
    x = lax.rem(dp, 4)
    y = lax.rem(lax.div(sq, 2), 4)
    z = lax.div(dp, 4) * 2 + lax.div(sq, 8)
    return x, y, z, lax.rem(sq, 2)


def device(x, y, z, c):
    return (lax.div(z, 2) * 4 + x, lax.rem(z, 2) * 8 + y * 2 + c)


def project_kernel(
    x_ref, w_ref, qkv_ref, wo_ref, xbuf, wbuf, pbuf, zbuf, pack, ssem, rsem, lsem
):
    x, y, z, c = place()
    zl = lax.rem(z, 2)
    xp, xm, x2 = lax.rem(x + 1, 4), lax.rem(x + 3, 4), lax.rem(x + 2, 4)
    yp, ym, y2 = lax.rem(y + 1, 4), lax.rem(y + 3, 4), lax.rem(y + 2, 4)
    co = 1 - c
    mate = z + 1 - 2 * zl
    to_x = [device(xx, y, z, c) for xx in (xp, xm, x2)]
    to_y = [device(x, yy, z, c) for yy in (yp, ym, y2)]
    to_z = {d: device(x, y, lax.rem(z + d, 8), c) for d in range(1, 8)}
    to_co, to_mate = device(x, y, z, co), device(x, y, mate, c)

    barrier = pltpu.get_barrier_semaphore()
    for to in (*to_x, *to_y, *to_z.values(), to_co):
        pl.semaphore_signal(barrier, inc=1, device_id=to, device_id_type=MESH)
    pl.semaphore_wait(barrier, 14)

    sent, names, local = [], {}, []

    def sem(*name):
        return names.setdefault(name, len(names))

    def copy(src, dst, k, to):
        return pltpu.make_async_remote_copy(
            src_ref=src,
            dst_ref=dst,
            send_sem=ssem.at[k],
            recv_sem=rsem.at[k],
            device_id=to,
            device_id_type=MESH,
        )

    def send(src, dst, to, *name):
        cp = copy(src, dst, sem(*name), to)
        cp.start()
        sent.append(cp)

    def arrived(dst, *name):
        copy(dst, dst, sem(*name), to_co).wait_recv()

    def keep(src, dst):
        cp = pltpu.make_async_copy(src, dst, lsem.at[len(local)])
        cp.start()
        local.append(cp)
        return cp

    def behind(d):
        return lax.rem(z + 8 - d, 8)

    def wslot(zz, xx):
        row = pl.multiple_of((lax.div(zz, 2) * 4 + xx) * HD, 16)
        return wbuf.at[lax.rem(zz, 2), pl.ds(row, HD), :]

    half = ROWS // 2

    def xpart(cc, yy, part):
        return xbuf.at[cc, yy, pl.ds(part * half, half), :]

    w_mine, wo_mine = w_ref.at[:, 0:PACK], w_ref.at[:, PACK : PACK + 128]
    for d in (1, 7, 3, 5, 2, 6, 4):
        send(w_mine, wslot(z, x), to_z[d], "wz", d)
    for to, k in zip(to_x, range(3)):
        send(w_mine, wslot(z, x), to, "wx", 0, k)
    for d in (1, 7, 2, 6, 3, 5, 4):
        send(wo_mine, zbuf.at[z], to_z[d], "oz", d)
    for part in (0, 1):
        src = x_ref.at[pl.ds(part * half, half), :]
        send(src, xpart(c, y, part), to_y[0], "y+", part)
        src = x_ref.at[pl.ds((1 - part) * half, half), :]
        send(src, xpart(c, y, 1 - part), to_y[1], "y-", 1 - part)
    send(x_ref, xbuf.at[c, y], to_co, "c", 0)
    own_x = keep(x_ref, xbuf.at[c, y])
    own_w = keep(w_mine, wslot(z, x))
    own_o = keep(wo_mine, zbuf.at[z])

    for d in (1, 7, 3, 5, 2, 6, 4):
        here = wslot(behind(d), x)
        arrived(here, "wz", d)
        for to, k in zip(to_x, range(3)):
            send(here, here, to, "wx", d, k)

    for d in range(1, 8):
        arrived(zbuf.at[behind(d)], "oz", d)
    own_o.wait()
    for zz in range(8):
        lane = (zz % 2) * 4 * HD + (zz // 2) * HD
        pack[:, lane : lane + HD] = zbuf[zz][:, :HD]
    for to, k in zip(to_y, range(3)):
        send(pack, wo_ref.at[c, x, y], to, "oy", k)
    own_pack = keep(pack, wo_ref.at[c, x, y])

    arrived(xpart(c, ym, 0), "y+", 0)
    send(xpart(c, ym, 0), xpart(c, ym, 0), to_y[0], "y2", 0)
    arrived(xpart(c, yp, 1), "y-", 1)
    send(xpart(c, yp, 1), xpart(c, yp, 1), to_y[1], "y2", 1)

    def w_here(ds):
        for d in ds:
            for k, xx in enumerate((xm, xp, x2)):
                arrived(wslot(behind(d), xx), "wx", d, k)

    def block(lo, cc, yy):
        row = pl.multiple_of((lo * 8 + yy * 2 + cc) * ROWS, ROWS)
        return qkv_ref.at[pl.ds(row, ROWS), :]

    places = ((c, y), (co, y), (c, ym), (c, yp), (co, ym), (co, yp), (c, y2), (co, y2))

    def project(i, whose):
        head = zl if whose else 1 - zl
        cc, yy = places[i]
        pbuf[i, whose] = jnp.dot(
            xbuf[cc, yy], wbuf[head], preferred_element_type=F32
        ).astype(BF16)
        if whose:
            keep(pbuf.at[i, 1], block(zl, cc, yy))
        else:
            send(pbuf.at[i, 0], block(zl, cc, yy), to_mate, "mate", i)

    w_here((1, 7, 3, 5))
    own_x.wait()
    project(0, 0)
    arrived(xbuf.at[co, y], "c", 0)
    project(1, 0)
    own_w.wait()
    w_here((0, 2, 6, 4))
    project(0, 1)
    project(1, 1)

    own_pack.wait()
    for k, yy in enumerate((y, ym, yp, y2)):
        here = wo_ref.at[c, x, yy]
        if k:
            arrived(here, "oy", k - 1)
        send(here, here, to_x[0], "ox", k, 0)
        send(here, here, to_x[1], "ox", k, 1)

    arrived(xpart(c, ym, 1), "y+", 1)
    send(xbuf.at[c, ym], xbuf.at[c, ym], to_co, "c", 1)
    arrived(xpart(c, yp, 0), "y-", 0)
    send(xbuf.at[c, yp], xbuf.at[c, yp], to_co, "c", 2)
    project(2, 0)
    project(3, 0)
    arrived(xbuf.at[co, ym], "c", 1)
    project(4, 0)
    arrived(xbuf.at[co, yp], "c", 2)
    project(5, 0)
    for i in (2, 3, 4, 5):
        project(i, 1)

    for k, yy in enumerate((y, ym, yp, y2)):
        side = k % 2
        here = wo_ref.at[c, (xm, xp)[side], yy]
        arrived(here, "ox", k, side)
        send(here, here, to_x[side], "ox", k, 2)

    arrived(xpart(c, y2, 0), "y2", 0)
    arrived(xpart(c, y2, 1), "y2", 1)
    send(xbuf.at[c, y2], xbuf.at[c, y2], to_co, "c", 3)
    project(6, 0)
    arrived(xbuf.at[co, y2], "c", 3)
    project(7, 0)
    project(6, 1)
    project(7, 1)

    send(wo_ref.at[c, x], wo_ref.at[c, x], to_co, "oc", 0)
    for k, yy in enumerate((y, ym, yp, y2)):
        side = 1 - k % 2
        arrived(wo_ref.at[c, (xm, xp)[side], yy], "ox", k, side)
    send(wo_ref.at[c, xm], wo_ref.at[c, xm], to_co, "oc", 1)
    send(wo_ref.at[c, xp], wo_ref.at[c, xp], to_co, "oc", 2)
    for k, yy in enumerate((y, ym, yp, y2)):
        arrived(wo_ref.at[c, x2, yy], "ox", k, 2)
    send(wo_ref.at[c, x2], wo_ref.at[c, x2], to_co, "oc", 3)
    for i, (cc, yy) in enumerate(places):
        arrived(block(1 - zl, cc, yy), "mate", i)
    for k, xx in enumerate((x, xm, xp, x2)):
        arrived(wo_ref.at[co, xx], "oc", k)
    for cp in local[4:]:
        cp.wait()
    for cp in sent:
        cp.wait_send()


def project(patches, w):
    return pl.pallas_call(
        project_kernel,
        out_shape=(
            jax.ShapeDtypeStruct((SEQ, PACK), BF16),
            jax.ShapeDtypeStruct((2, 4, 4, HD, 8 * HD), BF16),
        ),
        in_specs=[
            pl.BlockSpec(memory_space=pl.ANY),
            pl.BlockSpec(memory_space=pltpu.VMEM),
        ],
        out_specs=(pl.BlockSpec(memory_space=pl.ANY),) * 2,
        scratch_shapes=[
            pltpu.VMEM((2, 4, ROWS, D), BF16),
            pltpu.VMEM((2, D, PACK), BF16),
            pltpu.VMEM((8, 2, ROWS, PACK), BF16),
            pltpu.VMEM((8, HD, 128), BF16),
            pltpu.VMEM((HD, 8 * HD), BF16),
            pltpu.SemaphoreType.DMA((80,)),
            pltpu.SemaphoreType.DMA((80,)),
            pltpu.SemaphoreType.DMA((16,)),
        ],
        compiler_params=pltpu.CompilerParams(
            collective_id=0, has_side_effects=True, vmem_limit_bytes=40 << 20
        ),
        name="project",
    )(patches, w)


TQ = 256
CK = 768
SUB = 128
BLOCKS = SEQ // TQ
SCALE = math.log2(math.e) / math.sqrt(HD)


def rows_fold(op, a):
    parts = [a[i : i + 8] for i in range(0, a.shape[0], 8)]
    while len(parts) > 1:
        odd = parts[len(parts) // 2 * 2 :]
        parts = [op(l, r) for l, r in zip(parts[::2], parts[1::2])] + odd
    return parts[0]


def attend_kernel(
    ids_ref, qkv_ref, o_ref, kaug, qaug, vt, s0, s1, e0, e1, acc, state
):
    ids = ids_ref[...]
    cuts = [jnp.sum((ids < a).astype(F32)).astype(jnp.int32) for a in (1, 2, 3)]

    def image_of(pos):
        return sum((pos >= cut).astype(jnp.int32) for cut in cuts)

    lane = lax.broadcasted_iota(jnp.int32, (TQ, 128), 1)
    kpos = lax.broadcasted_iota(jnp.int32, (TQ, 128), 0)
    mark = lax.broadcasted_iota(jnp.int32, (128 - HD, TQ), 0)
    qpos = lax.broadcasted_iota(jnp.int32, (128 - HD, TQ), 1)

    @pl.loop(0, BLOCKS)
    def _(i):
        rows = pl.ds(pl.multiple_of(i * TQ, TQ), TQ)
        other = image_of(kpos + i * TQ) != lane - HD
        kaug[rows, :] = jnp.where(
            lane < HD, qkv_ref[rows, 128:256], jnp.where(other, 1.0, 0.0).astype(BF16)
        )
        turned = qkv_ref[rows, :].T
        own = image_of(qpos + i * TQ) == mark
        qaug[0:HD, rows] = turned[0:HD]
        qaug[HD:128, rows] = jnp.where(own, -1e30, 0.0).astype(BF16)
        vt[0:48, rows] = turned[80:128]
        vt[48:80, rows] = turned[208:240]

    kaug[SEQ : SEQ + CK, :] = jnp.ones((CK, 128), BF16)
    vt[:, SEQ : SEQ + CK] = jnp.zeros((HD, CK), BF16)
    for ref in (s0, s1, e0, e1, acc, state):
        ref[...] = jnp.zeros_like(ref)

    def span(i):
        first = i * TQ
        lo, hi = jnp.int32(0), jnp.int32(SEQ)
        for cut in cuts:
            lo = jnp.maximum(lo, jnp.where(cut <= first, cut, 0))
            hi = jnp.minimum(hi, jnp.where(cut >= first + TQ, cut, SEQ))
        lo = lax.div(lo, 128) * 128
        return lo, lax.div(hi - lo + CK - 1, CK)

    steps = lax.fori_loop(0, BLOCKS, lambda i, n: n + span(i)[1], jnp.int32(0))

    def step(s_new, s_old, e_old, e_new, carry):
        i1, k1, i2, k2, i3, k3, first2, first3 = carry
        high, top = state[0:1, :], state[8:9, :]
        rescale3, total = state[16:17, :], state[24:32, :]
        before = jnp.where(first2 > 0, -jnp.inf, top)
        top = jnp.maximum(before, high)
        rescale2 = jnp.exp2((before - top) * SCALE)
        block1 = jnp.minimum(i1, BLOCKS - 1)
        query = qaug[:, pl.ds(pl.multiple_of(block1 * TQ, TQ), TQ)]
        highs, sums = [], []
        for u in range(0, CK, SUB):
            part = slice(u, u + SUB)
            keys = kaug[pl.ds(pl.multiple_of(k1 + u, 128), SUB), :]
            s = jnp.dot(keys, query, preferred_element_type=F32)
            s_new[part, :] = s
            highs.append(rows_fold(jnp.maximum, s))
            e = jnp.exp2((s_old[part, :] - top) * SCALE)
            sums.append(rows_fold(jnp.add, e))
            e_new[part, :] = e.astype(BF16)
            if u == 0:
                values = vt[:, pl.ds(pl.multiple_of(k3, 128), CK)]
                mixed = jnp.dot(values, e_old[...], preferred_element_type=F32)
        mixed = acc[...] * rescale3 + mixed
        acc[...] = mixed
        inverse = 1.0 / jnp.sum(total, axis=0, keepdims=True)
        out = pl.ds(pl.multiple_of(i3 * TQ, TQ), TQ)
        o_ref[:, out] = (mixed * inverse).astype(BF16)
        state[0:1, :] = jnp.max(
            functools.reduce(jnp.maximum, highs), axis=0, keepdims=True
        )
        state[8:9, :] = top
        state[16:17, :] = rescale2
        state[24:32, :] = total * rescale2 + functools.reduce(jnp.add, sums)
        lo, n = span(block1)
        first1 = jnp.where(k1 == lo, 1, 0)
        last1 = jnp.where(k1 + CK >= lo + n * CK, 1, 0)
        following = jnp.minimum(i1 + last1, BLOCKS)
        start = span(jnp.minimum(following, BLOCKS - 1))[0]
        k_next = jnp.where(last1 > 0, start, k1 + CK)
        return following, k_next, i1, k1, i2, k2, first1, first2

    def pair(_, carry):
        carry = step(s0, s1, e0, e1, carry)
        return step(s1, s0, e1, e0, carry)

    lax.fori_loop(0, lax.div(steps + 3, 2), pair, (jnp.int32(0),) * 8)


def attend(ids, qkv):
    return pl.pallas_call(
        attend_kernel,
        out_shape=jax.ShapeDtypeStruct((HD, SEQ + TQ), BF16),
        in_specs=[pl.BlockSpec(memory_space=pltpu.VMEM)] * 2,
        out_specs=pl.BlockSpec(memory_space=pltpu.VMEM),
        scratch_shapes=[
            pltpu.VMEM((SEQ + CK, 128), BF16),
            pltpu.VMEM((128, SEQ), BF16),
            pltpu.VMEM((HD, SEQ + CK), BF16),
            pltpu.VMEM((CK, TQ), F32),
            pltpu.VMEM((CK, TQ), F32),
            pltpu.VMEM((CK, TQ), BF16),
            pltpu.VMEM((CK, TQ), BF16),
            pltpu.VMEM((HD, TQ), F32),
            pltpu.VMEM((32, TQ), F32),
        ],
        compiler_params=pltpu.CompilerParams(vmem_limit_bytes=40 << 20),
        name="attend",
    )(ids, qkv)


def output_kernel(o_ref, wg_ref, out_ref, held, whole, ssem, rsem):
    dp, me = lax.axis_index("dp"), lax.axis_index("seq")
    barrier = pltpu.get_barrier_semaphore()
    for k in range(1, 16):
        to = (dp, lax.rem(me + k, 16))
        pl.semaphore_signal(barrier, inc=1, device_id=to, device_id_type=MESH)
    pl.semaphore_wait(barrier, 15)

    def mine(k):
        cols = pl.ds(pl.multiple_of(lax.rem(me + k, 16) * ROWS, ROWS), ROWS)
        return o_ref.at[:, cols]

    def slot(s):
        return held.at[pl.ds(pl.multiple_of(s * HD, 16), HD), :]

    copies = []
    for k in range(1, 16):
        cp = pltpu.make_async_remote_copy(
            src_ref=mine(k),
            dst_ref=slot(me),
            send_sem=ssem.at[k],
            recv_sem=rsem.at[k],
            device_id=(dp, lax.rem(me + k, 16)),
            device_id_type=MESH,
        )
        cp.start()
        copies.append(cp)
    own = pltpu.make_async_copy(mine(0), slot(me), ssem.at[0])
    own.start()

    @pl.loop(0, 8)
    def _(i):
        for zl, x, zh in itertools.product(range(2), range(4), range(4)):
            row = pl.multiple_of((zl * 8 + i) * HD, 16)
            col, lane = (zh * 4 + x) * HD, (zl * 4 + zh) * HD
            whole[pl.ds(row, HD), col : col + HD] = wg_ref[
                lax.rem(i, 2), x, lax.div(i, 2), :, lane : lane + HD
            ]

    own.wait()
    for k in range(1, 16):
        frm = slot(lax.rem(me + 16 - k, 16))
        pltpu.make_async_remote_copy(
            src_ref=frm,
            dst_ref=frm,
            send_sem=ssem.at[k],
            recv_sem=rsem.at[k],
            device_id=(dp, lax.rem(me + k, 16)),
            device_id_type=MESH,
        ).wait_recv()
    out_ref[...] = lax.dot_general(
        held[...], whole[...], (((0,), (0,)), ((), ())), preferred_element_type=F32
    ).astype(BF16)
    for cp in copies:
        cp.wait_send()


def output(o, wg):
    return pl.pallas_call(
        output_kernel,
        out_shape=jax.ShapeDtypeStruct((ROWS, D), BF16),
        in_specs=[pl.BlockSpec(memory_space=pltpu.VMEM)] * 2,
        out_specs=pl.BlockSpec(memory_space=pltpu.VMEM),
        scratch_shapes=[
            pltpu.VMEM((D, ROWS), BF16),
            pltpu.VMEM((D, D), BF16),
            pltpu.SemaphoreType.DMA((16,)),
            pltpu.SemaphoreType.DMA((16,)),
        ],
        compiler_params=pltpu.CompilerParams(
            collective_id=1, has_side_effects=True, vmem_limit_bytes=40 << 20
        ),
        name="output",
    )(o, wg)


def shards(patches, image_ids, w_qkv, w_out):
    q, k, v = w_qkv[0], w_qkv[1], w_qkv[2]
    spare = jnp.zeros((HD, PACK - 3 * HD), BF16)
    more = jnp.zeros((HD, 128 - HD), BF16)
    w = jnp.concatenate([q, v[:, :48], k, v[:, 48:], spare, w_out, more], axis=1)
    qkv, wo = project(patches[0], w)
    o = attend(image_ids.reshape(SEQ // 128, 128), qkv)
    out = output(o, wo)
    return out[None]


def solution(mesh):
    return jax.shard_map(
        shards,
        mesh=mesh,
        in_specs=(P("dp", "seq", None), P("dp", None), P(None, "dp", "seq"), P("seq", "dp")),
        out_specs=P("dp", "seq", None),
        check_vma=False,
    )
```

```python
import functools
import itertools
import math

import jax
import jax.numpy as jnp
from jax import lax
from jax.experimental import pallas as pl
from jax.experimental.pallas import tpu as pltpu
from jax.sharding import PartitionSpec as P

MESH = pl.DeviceIdType.MESH
HD = 80
D = 1280
ROWS = 256
SEQ = 4096
PACK = 256
TQ = 256
CK = 768
SUB = 128
BLOCKS = SEQ // TQ
SCALE = math.log2(math.e) / math.sqrt(HD)
BF16 = jnp.bfloat16
F32 = jnp.float32


def place():
    dp, sq = lax.axis_index("dp"), lax.axis_index("seq")
    x = lax.rem(dp, 4)
    y = lax.rem(lax.div(sq, 2), 4)
    z = lax.div(dp, 4) * 2 + lax.div(sq, 8)
    return x, y, z, lax.rem(sq, 2)


def device(x, y, z, c):
    return (lax.div(z, 2) * 4 + x, lax.rem(z, 2) * 8 + y * 2 + c)


def project_kernel(
    x_ref, ids_ref, wqkv_ref, wout_ref,
    kaug, qaug, vt, cut_ref, wo_ref,
    ids, wq, wo, mine, xbuf, wbuf, pbuf, qkv, zbuf, pack, ssem, rsem, lsem,
):
    x, y, z, c = place()
    zl = lax.rem(z, 2)
    xp, xm, x2 = lax.rem(x + 1, 4), lax.rem(x + 3, 4), lax.rem(x + 2, 4)
    yp, ym, y2 = lax.rem(y + 1, 4), lax.rem(y + 3, 4), lax.rem(y + 2, 4)
    co = 1 - c
    mate = z + 1 - 2 * zl
    to_x = [device(xx, y, z, c) for xx in (xp, xm, x2)]
    to_y = [device(x, yy, z, c) for yy in (yp, ym, y2)]
    to_z = {d: device(x, y, lax.rem(z + d, 8), c) for d in range(1, 8)}
    to_co, to_mate = device(x, y, z, co), device(x, y, mate, c)

    barrier = pltpu.get_barrier_semaphore()
    for to in (*to_x, *to_y, *to_z.values(), to_co):
        pl.semaphore_signal(barrier, inc=1, device_id=to, device_id_type=MESH)

    sent, names, local = [], {}, []

    def sem(*name):
        return names.setdefault(name, len(names))

    def copy(src, dst, k, to):
        return pltpu.make_async_remote_copy(
            src_ref=src,
            dst_ref=dst,
            send_sem=ssem.at[k],
            recv_sem=rsem.at[k],
            device_id=to,
            device_id_type=MESH,
        )

    def send(src, dst, to, *name):
        cp = copy(src, dst, sem(*name), to)
        cp.start()
        sent.append(cp)

    def arrived(dst, *name):
        copy(dst, dst, sem(*name), to_co).wait_recv()

    def keep(src, dst):
        cp = pltpu.make_async_copy(src, dst, lsem.at[len(local)])
        cp.start()
        local.append(cp)
        return cp

    loads = (
        keep(wqkv_ref, wq), keep(wout_ref, wo), keep(x_ref, xbuf.at[c, y]),
        keep(ids_ref, ids),
    )
    loads[0].wait()
    loads[1].wait()
    mine[:, 0:80] = wq[0]
    mine[:, 80:128] = wq[2][:, :48]
    mine[:, 128:208] = wq[1]
    mine[:, 208:240] = wq[2][:, 48:]
    mine[:, 240:256] = jnp.zeros((HD, 16), BF16)
    mine[:, 256:336] = wo[...]
    pl.semaphore_wait(barrier, 14)

    def behind(d):
        return lax.rem(z + 8 - d, 8)

    def lanes(part):
        return slice(0, PACK) if part is None else slice(part * 128, part * 128 + 128)

    def wslot(zz, xx, part=None):
        row = pl.multiple_of((lax.div(zz, 2) * 4 + xx) * HD, 16)
        return wbuf.at[lax.rem(zz, 2), pl.ds(row, HD), lanes(part)]

    half = ROWS // 2

    def xpart(cc, yy, part):
        return xbuf.at[cc, yy, pl.ds(part * half, half), :]

    theirs, ours = (1, 7, 3, 5), (2, 6, 4)
    wo_mine = mine.at[:, PACK : PACK + 128]

    def w_mine(part=None):
        return mine.at[:, lanes(part)]

    for part in (0, 1):
        for d in theirs:
            send(w_mine(part), wslot(z, x, part), to_z[d], "wz", d, part)
    for part in (0, 1):
        src = x_ref.at[pl.ds(part * half, half), :]
        send(src, xpart(c, y, part), to_y[0], "y+", part)
        src = x_ref.at[pl.ds((1 - part) * half, half), :]
        send(src, xpart(c, y, 1 - part), to_y[1], "y-", 1 - part)
    send(x_ref, xbuf.at[c, y], to_co, "c", 0)
    for d in ours:
        send(w_mine(), wslot(z, x), to_z[d], "wz", d, None)
    for d in (1, 7, 2, 6, 3, 5, 4):
        send(wo_mine, zbuf.at[z], to_z[d], "oz", d)
    own_w = keep(w_mine(), wslot(z, x))
    own_o = keep(wo_mine, zbuf.at[z])

    def along_x(src, d, part):
        for to, k in zip(to_x, range(3)):
            send(src, wslot(behind(d), x, part), to, "wx", d, part, k)

    for part in (0, 1):
        for d in theirs:
            here = wslot(behind(d), x, part)
            arrived(here, "wz", d, part)
            along_x(here, d, part)
    along_x(w_mine(), 0, None)
    for d in ours:
        here = wslot(behind(d), x)
        arrived(here, "wz", d, None)
        along_x(here, d, None)

    def w_here(ds, part):
        for d in ds:
            for k, xx in enumerate((xm, xp, x2)):
                arrived(wslot(behind(d), xx, part), "wx", d, part, k)

    places = ((c, y), (co, y), (c, ym), (c, yp), (co, ym), (co, yp), (c, y2), (co, y2))

    def block(lo, i):
        cc, yy = places[i]
        return lo * 8 + yy * 2 + cc

    def give(i, part=None):
        cc, yy = places[i]
        at = lanes(part)
        pbuf[i, :, at] = jnp.dot(
            xbuf[cc, yy], wbuf[1 - zl, :, at], preferred_element_type=F32
        ).astype(BF16)
        dst = qkv.at[block(zl, i), :, at]
        send(pbuf.at[i, :, at], dst, to_mate, "mate", i, part)

    lane = lax.broadcasted_iota(jnp.int32, (ROWS, 128), 1)
    kpos = lax.broadcasted_iota(jnp.int32, (ROWS, 128), 0)
    mark = lax.broadcasted_iota(jnp.int32, (128 - HD, ROWS), 0)
    qpos = lax.broadcasted_iota(jnp.int32, (128 - HD, ROWS), 1)
    cuts = []

    def image_of(pos):
        return sum((pos >= cut).astype(jnp.int32) for cut in cuts)

    def lay_out(b, heads):
        rows = pl.ds(pl.multiple_of(b * ROWS, ROWS), ROWS)
        other = image_of(kpos + b * ROWS) != lane - HD
        kaug[rows, :] = jnp.where(
            lane < HD, heads[:, 128:256], jnp.where(other, 1.0, 0.0).astype(BF16)
        )
        turned = heads.T
        own = image_of(qpos + b * ROWS) == mark
        qaug[0:HD, rows] = turned[0:HD]
        qaug[HD:128, rows] = jnp.where(own, -1e30, 0.0).astype(BF16)
        vt[0:48, rows] = turned[80:128]
        vt[48:80, rows] = turned[208:240]

    def take(i):
        cc, yy = places[i]
        heads = jnp.dot(
            xbuf[cc, yy], wbuf[zl], preferred_element_type=F32
        ).astype(BF16)
        lay_out(block(zl, i), heads)

    def receive(i, parts=(None,)):
        b = block(1 - zl, i)
        for part in parts:
            arrived(qkv.at[b, :, lanes(part)], "mate", i, part)
        lay_out(b, qkv[b])

    loads[2].wait()
    w_here(theirs, 0)
    give(0, 0)
    arrived(xbuf.at[co, y], "c", 0)
    give(1, 0)

    for d in range(1, 8):
        arrived(zbuf.at[behind(d)], "oz", d)
    own_o.wait()
    for zz in range(8):
        lane0 = (zz % 2) * 4 * HD + (zz // 2) * HD
        pack[:, lane0 : lane0 + HD] = zbuf[zz][:, :HD]
    for to, k in zip(to_y, range(3)):
        send(pack, wo_ref.at[c, x, y], to, "oy", k)
    own_pack = keep(pack, wo_ref.at[c, x, y])

    arrived(xpart(c, ym, 0), "y+", 0)
    send(xpart(c, ym, 0), xpart(c, ym, 0), to_y[0], "y2", 0)
    arrived(xpart(c, yp, 1), "y-", 1)
    send(xpart(c, yp, 1), xpart(c, yp, 1), to_y[1], "y2", 1)

    w_here(theirs, 1)
    give(0, 1)
    give(1, 1)
    loads[3].wait()
    for a in (1, 2, 3):
        count = jnp.sum((ids[...] < a).astype(F32))
        cuts.append(count.astype(jnp.int32))
        cut_ref[a - 1 : a, :] = jnp.full((1, 128), count, F32)
    cut_ref[3:8, :] = jnp.zeros((5, 128), F32)
    kaug[SEQ : SEQ + CK, :] = jnp.ones((CK, 128), BF16)
    vt[:, SEQ : SEQ + CK] = jnp.zeros((HD, CK), BF16)
    own_w.wait()
    w_here((0, *ours), None)
    take(0)
    take(1)

    own_pack.wait()
    for k, yy in enumerate((y, ym, yp, y2)):
        here = wo_ref.at[c, x, yy]
        if k:
            arrived(here, "oy", k - 1)
        send(here, here, to_x[0], "ox", k, 0)
        send(here, here, to_x[1], "ox", k, 1)

    arrived(xpart(c, ym, 1), "y+", 1)
    send(xbuf.at[c, ym], xbuf.at[c, ym], to_co, "c", 1)
    arrived(xpart(c, yp, 0), "y-", 0)
    send(xbuf.at[c, yp], xbuf.at[c, yp], to_co, "c", 2)
    give(2)
    give(3)
    arrived(xbuf.at[co, ym], "c", 1)
    give(4)
    arrived(xbuf.at[co, yp], "c", 2)
    give(5)
    for i in (2, 3, 4, 5):
        take(i)

    for k, yy in enumerate((y, ym, yp, y2)):
        side = k % 2
        here = wo_ref.at[c, (xm, xp)[side], yy]
        arrived(here, "ox", k, side)
        send(here, here, to_x[side], "ox", k, 2)

    arrived(xpart(c, y2, 0), "y2", 0)
    arrived(xpart(c, y2, 1), "y2", 1)
    send(xbuf.at[c, y2], xbuf.at[c, y2], to_co, "c", 3)
    give(6)
    arrived(xbuf.at[co, y2], "c", 3)
    give(7)
    take(6)
    take(7)
    receive(0, (0, 1))
    receive(1, (0, 1))

    send(wo_ref.at[c, x], wo_ref.at[c, x], to_co, "oc", 0)
    for k, yy in enumerate((y, ym, yp, y2)):
        side = 1 - k % 2
        arrived(wo_ref.at[c, (xm, xp)[side], yy], "ox", k, side)
    send(wo_ref.at[c, xm], wo_ref.at[c, xm], to_co, "oc", 1)
    send(wo_ref.at[c, xp], wo_ref.at[c, xp], to_co, "oc", 2)
    for k, yy in enumerate((y, ym, yp, y2)):
        arrived(wo_ref.at[c, x2, yy], "ox", k, 2)
    send(wo_ref.at[c, x2], wo_ref.at[c, x2], to_co, "oc", 3)
    for i in range(2, 8):
        receive(i)
    for k, xx in enumerate((x, xm, xp, x2)):
        arrived(wo_ref.at[co, xx], "oc", k)
    for cp in sent:
        cp.wait_send()


def project(patches, ids, w_qkv, w_out):
    return pl.pallas_call(
        project_kernel,
        out_shape=(
            jax.ShapeDtypeStruct((SEQ + CK, 128), BF16),
            jax.ShapeDtypeStruct((128, SEQ), BF16),
            jax.ShapeDtypeStruct((HD, SEQ + CK), BF16),
            jax.ShapeDtypeStruct((8, 128), F32),
            jax.ShapeDtypeStruct((2, 4, 4, HD, 8 * HD), BF16),
        ),
        in_specs=[pl.BlockSpec(memory_space=pltpu.HBM)] * 4,
        out_specs=(pl.BlockSpec(memory_space=pltpu.VMEM),) * 4
        + (pl.BlockSpec(memory_space=pl.ANY),),
        scratch_shapes=[
            pltpu.VMEM((SEQ // 128, 128), jnp.int32),
            pltpu.VMEM((3, HD, HD), BF16),
            pltpu.VMEM((HD, HD), BF16),
            pltpu.VMEM((HD, PACK + 128), BF16),
            pltpu.VMEM((2, 4, ROWS, D), BF16),
            pltpu.VMEM((2, D, PACK), BF16),
            pltpu.VMEM((8, ROWS, PACK), BF16),
            pltpu.VMEM((16, ROWS, PACK), BF16),
            pltpu.VMEM((8, HD, 128), BF16),
            pltpu.VMEM((HD, 8 * HD), BF16),
            pltpu.SemaphoreType.DMA((100,)),
            pltpu.SemaphoreType.DMA((100,)),
            pltpu.SemaphoreType.DMA((8,)),
        ],
        compiler_params=pltpu.CompilerParams(
            collective_id=0, has_side_effects=True, vmem_limit_bytes=40 << 20
        ),
        name="project",
    )(patches, ids, w_qkv, w_out)


def rows_fold(op, a):
    parts = [a[i : i + 8] for i in range(0, a.shape[0], 8)]
    while len(parts) > 1:
        odd = parts[len(parts) // 2 * 2 :]
        parts = [op(l, r) for l, r in zip(parts[::2], parts[1::2])] + odd
    return parts[0]


def attend_kernel(
    cut_ref, kaug, qaug, vt, o_ref, s0, s1, e0, e1, acc, state
):
    cuts = [jnp.max(cut_ref[a : a + 1, :]).astype(jnp.int32) for a in range(3)]
    for ref in (s0, s1, e0, e1, acc, state):
        ref[...] = jnp.zeros_like(ref)

    def span(i):
        first = i * TQ
        lo, hi = jnp.int32(0), jnp.int32(SEQ)
        for cut in cuts:
            lo = jnp.maximum(lo, jnp.where(cut <= first, cut, 0))
            hi = jnp.minimum(hi, jnp.where(cut >= first + TQ, cut, SEQ))
        lo = lax.div(lo, 128) * 128
        return lo, lax.div(hi - lo + CK - 1, CK)

    steps = lax.fori_loop(0, BLOCKS, lambda i, n: n + span(i)[1], jnp.int32(0))

    def step(s_new, s_old, e_old, e_new, carry):
        i1, k1, i2, k2, i3, k3, first2, first3 = carry
        high, top = state[0:1, :], state[8:9, :]
        rescale3, total = state[16:17, :], state[24:32, :]
        before = jnp.where(first2 > 0, -jnp.inf, top)
        top = jnp.maximum(before, high)
        rescale2 = jnp.exp2((before - top) * SCALE)
        block1 = jnp.minimum(i1, BLOCKS - 1)
        query = qaug[:, pl.ds(pl.multiple_of(block1 * TQ, TQ), TQ)]
        highs, sums = [], []
        for u in range(0, CK, SUB):
            part = slice(u, u + SUB)
            keys = kaug[pl.ds(pl.multiple_of(k1 + u, 128), SUB), :]
            s = jnp.dot(keys, query, preferred_element_type=F32)
            s_new[part, :] = s
            highs.append(rows_fold(jnp.maximum, s))
            e = jnp.exp2((s_old[part, :] - top) * SCALE)
            sums.append(rows_fold(jnp.add, e))
            e_new[part, :] = e.astype(BF16)
            if u == 0:
                values = vt[:, pl.ds(pl.multiple_of(k3, 128), CK)]
                mixed = jnp.dot(values, e_old[...], preferred_element_type=F32)
        mixed = acc[...] * rescale3 + mixed
        acc[...] = mixed
        inverse = 1.0 / jnp.sum(total, axis=0, keepdims=True)
        out = pl.ds(pl.multiple_of(i3 * TQ, TQ), TQ)
        o_ref[:, out] = (mixed * inverse).astype(BF16)
        state[0:1, :] = jnp.max(
            functools.reduce(jnp.maximum, highs), axis=0, keepdims=True
        )
        state[8:9, :] = top
        state[16:17, :] = rescale2
        state[24:32, :] = total * rescale2 + functools.reduce(jnp.add, sums)
        lo, n = span(block1)
        first1 = jnp.where(k1 == lo, 1, 0)
        last1 = jnp.where(k1 + CK >= lo + n * CK, 1, 0)
        following = jnp.minimum(i1 + last1, BLOCKS)
        start = span(jnp.minimum(following, BLOCKS - 1))[0]
        k_next = jnp.where(last1 > 0, start, k1 + CK)
        return following, k_next, i1, k1, i2, k2, first1, first2

    def pair(_, carry):
        carry = step(s0, s1, e0, e1, carry)
        return step(s1, s0, e1, e0, carry)

    lax.fori_loop(0, lax.div(steps + 3, 2), pair, (jnp.int32(0),) * 8)


def attend(cuts, kaug, qaug, vt):
    return pl.pallas_call(
        attend_kernel,
        out_shape=jax.ShapeDtypeStruct((HD, SEQ + TQ), BF16),
        in_specs=[pl.BlockSpec(memory_space=pltpu.VMEM)] * 4,
        out_specs=pl.BlockSpec(memory_space=pltpu.VMEM),
        scratch_shapes=[
            pltpu.VMEM((CK, TQ), F32),
            pltpu.VMEM((CK, TQ), F32),
            pltpu.VMEM((CK, TQ), BF16),
            pltpu.VMEM((CK, TQ), BF16),
            pltpu.VMEM((HD, TQ), F32),
            pltpu.VMEM((32, TQ), F32),
        ],
        compiler_params=pltpu.CompilerParams(vmem_limit_bytes=40 << 20),
        name="attend",
    )(cuts, kaug, qaug, vt)


def output_kernel(o_ref, wg_ref, out_ref, held, whole, ssem, rsem):
    dp, me = lax.axis_index("dp"), lax.axis_index("seq")
    barrier = pltpu.get_barrier_semaphore()
    for k in range(1, 16):
        to = (dp, lax.rem(me + k, 16))
        pl.semaphore_signal(barrier, inc=1, device_id=to, device_id_type=MESH)
    pl.semaphore_wait(barrier, 15)

    def mine(k):
        cols = pl.ds(pl.multiple_of(lax.rem(me + k, 16) * ROWS, ROWS), ROWS)
        return o_ref.at[:, cols]

    def slot(s):
        return held.at[pl.ds(pl.multiple_of(s * HD, 16), HD), :]

    copies = []
    for k in range(1, 16):
        cp = pltpu.make_async_remote_copy(
            src_ref=mine(k),
            dst_ref=slot(me),
            send_sem=ssem.at[k],
            recv_sem=rsem.at[k],
            device_id=(dp, lax.rem(me + k, 16)),
            device_id_type=MESH,
        )
        cp.start()
        copies.append(cp)
    own = pltpu.make_async_copy(mine(0), slot(me), ssem.at[0])
    own.start()

    @pl.loop(0, 8)
    def _(i):
        for zl, x, zh in itertools.product(range(2), range(4), range(4)):
            row = pl.multiple_of((zl * 8 + i) * HD, 16)
            col, lane = (zh * 4 + x) * HD, (zl * 4 + zh) * HD
            whole[pl.ds(row, HD), col : col + HD] = wg_ref[
                lax.rem(i, 2), x, lax.div(i, 2), :, lane : lane + HD
            ]

    own.wait()
    for k in range(1, 16):
        frm = slot(lax.rem(me + 16 - k, 16))
        pltpu.make_async_remote_copy(
            src_ref=frm,
            dst_ref=frm,
            send_sem=ssem.at[k],
            recv_sem=rsem.at[k],
            device_id=(dp, lax.rem(me + k, 16)),
            device_id_type=MESH,
        ).wait_recv()
    out_ref[...] = lax.dot_general(
        held[...], whole[...], (((0,), (0,)), ((), ())), preferred_element_type=F32
    ).astype(BF16)
    for cp in copies:
        cp.wait_send()


def output(o, wg):
    return pl.pallas_call(
        output_kernel,
        out_shape=jax.ShapeDtypeStruct((ROWS, D), BF16),
        in_specs=[pl.BlockSpec(memory_space=pltpu.VMEM)] * 2,
        out_specs=pl.BlockSpec(memory_space=pltpu.VMEM),
        scratch_shapes=[
            pltpu.VMEM((D, ROWS), BF16),
            pltpu.VMEM((D, D), BF16),
            pltpu.SemaphoreType.DMA((16,)),
            pltpu.SemaphoreType.DMA((16,)),
        ],
        compiler_params=pltpu.CompilerParams(
            collective_id=1, has_side_effects=True, vmem_limit_bytes=40 << 20
        ),
        name="output",
    )(o, wg)


def shards(patches, image_ids, w_qkv, w_out):
    ids = image_ids.reshape(SEQ // 128, 128)
    kaug, qaug, vt, cuts, wo = project(patches[0], ids, w_qkv, w_out)
    o = attend(cuts, kaug, qaug, vt)
    out = output(o, wo)
    return out[None]


def solution(mesh):
    return jax.shard_map(
        shards,
        mesh=mesh,
        in_specs=(P("dp", "seq", None), P("dp", None), P(None, "dp", "seq"), P("seq", "dp")),
        out_specs=P("dp", "seq", None),
        check_vma=False,
    )
```

```python
import functools
import itertools
import math

import jax
import jax.numpy as jnp
from jax import lax
from jax.experimental import pallas as pl
from jax.experimental.pallas import tpu as pltpu
from jax.sharding import PartitionSpec as P

MESH = pl.DeviceIdType.MESH
HD = 80
D = 1280
ROWS = 256
SEQ = 4096
PACK = 256
TQ = 256
CK = 768
SUB = 128
BLOCKS = SEQ // TQ
SCALE = math.log2(math.e) / math.sqrt(HD)
BF16 = jnp.bfloat16
F32 = jnp.float32


def place():
    dp, sq = lax.axis_index("dp"), lax.axis_index("seq")
    x = lax.rem(dp, 4)
    y = lax.rem(lax.div(sq, 2), 4)
    z = lax.div(dp, 4) * 2 + lax.div(sq, 8)
    return x, y, z, lax.rem(sq, 2)


def device(x, y, z, c):
    return (lax.div(z, 2) * 4 + x, lax.rem(z, 2) * 8 + y * 2 + c)


def project_kernel(
    x_ref, ids_ref, wqkv_ref, wout_ref,
    kaug, qaug, vt, cut_ref, wo_ref,
    ids, wq, wo, mine, xbuf, wbuf, pbuf, qkv, zbuf, pack, ssem, rsem, lsem,
):
    x, y, z, c = place()
    zl = lax.rem(z, 2)
    xp, xm, x2 = lax.rem(x + 1, 4), lax.rem(x + 3, 4), lax.rem(x + 2, 4)
    yp, ym, y2 = lax.rem(y + 1, 4), lax.rem(y + 3, 4), lax.rem(y + 2, 4)
    co = 1 - c
    mate = z + 1 - 2 * zl
    to_x = [device(xx, y, z, c) for xx in (xp, xm, x2)]
    to_y = [device(x, yy, z, c) for yy in (yp, ym, y2)]
    to_z = {d: device(x, y, lax.rem(z + d, 8), c) for d in range(1, 8)}
    to_co, to_mate = device(x, y, z, co), device(x, y, mate, c)

    barrier = pltpu.get_barrier_semaphore()
    for to in (*to_x, *to_y, *to_z.values(), to_co):
        pl.semaphore_signal(barrier, inc=1, device_id=to, device_id_type=MESH)

    sent, names, local = [], {}, []

    def sem(*name):
        return names.setdefault(name, len(names))

    def copy(src, dst, k, to):
        return pltpu.make_async_remote_copy(
            src_ref=src,
            dst_ref=dst,
            send_sem=ssem.at[k],
            recv_sem=rsem.at[k],
            device_id=to,
            device_id_type=MESH,
        )

    def send(src, dst, to, *name):
        cp = copy(src, dst, sem(*name), to)
        cp.start()
        sent.append(cp)

    def arrived(dst, *name):
        copy(dst, dst, sem(*name), to_co).wait_recv()

    def keep(src, dst):
        cp = pltpu.make_async_copy(src, dst, lsem.at[len(local)])
        cp.start()
        local.append(cp)
        return cp

    loads = (
        keep(wqkv_ref, wq), keep(wout_ref, wo), keep(x_ref, xbuf.at[c, y]),
        keep(ids_ref, ids),
    )
    loads[0].wait()
    loads[1].wait()
    mine[:, 0:80] = wq[0]
    mine[:, 80:128] = wq[2][:, :48]
    mine[:, 128:208] = wq[1]
    mine[:, 208:240] = wq[2][:, 48:]
    mine[:, 240:256] = jnp.zeros((HD, 16), BF16)
    mine[:, 256:336] = wo[...]
    pl.semaphore_wait(barrier, 14)

    def behind(d):
        return lax.rem(z + 8 - d, 8)

    def lanes(part):
        return slice(0, PACK) if part is None else slice(part * 128, part * 128 + 128)

    def wslot(zz, xx, part=None):
        row = pl.multiple_of((lax.div(zz, 2) * 4 + xx) * HD, 16)
        return wbuf.at[lax.rem(zz, 2), pl.ds(row, HD), lanes(part)]

    half = ROWS // 2

    def xpart(cc, yy, part):
        return xbuf.at[cc, yy, pl.ds(part * half, half), :]

    theirs, ours = (1, 7, 3, 5), (2, 6, 4)
    wo_mine = mine.at[:, PACK : PACK + 128]

    def w_mine(part=None):
        return mine.at[:, lanes(part)]

    for part in (0, 1):
        for d in theirs:
            send(w_mine(part), wslot(z, x, part), to_z[d], "wz", d, part)
    for part in (0, 1):
        src = x_ref.at[pl.ds(part * half, half), :]
        send(src, xpart(c, y, part), to_y[0], "y+", part)
        send(src, xpart(c, y, part), to_y[1], "y-", part)
    send(x_ref, xbuf.at[c, y], to_co, "c", 0)
    for d in ours:
        send(w_mine(), wslot(z, x), to_z[d], "wz", d, None)
    for d in (1, 7, 2, 6, 3, 5, 4):
        send(wo_mine, zbuf.at[z], to_z[d], "oz", d)
    own_w = keep(w_mine(), wslot(z, x))
    own_o = keep(wo_mine, zbuf.at[z])

    def along_x(src, d, part):
        for to, k in zip(to_x, range(3)):
            send(src, wslot(behind(d), x, part), to, "wx", d, part, k)

    for part in (0, 1):
        for d in theirs:
            here = wslot(behind(d), x, part)
            arrived(here, "wz", d, part)
            along_x(here, d, part)
    along_x(w_mine(), 0, None)
    for d in ours:
        here = wslot(behind(d), x)
        arrived(here, "wz", d, None)
        along_x(here, d, None)

    def w_here(ds, part):
        for d in ds:
            for k, xx in enumerate((xm, xp, x2)):
                arrived(wslot(behind(d), xx, part), "wx", d, part, k)

    places = ((c, y), (co, y), (c, ym), (c, yp), (co, ym), (co, yp), (c, y2), (co, y2))

    def block(lo, i):
        cc, yy = places[i]
        return lo * 8 + yy * 2 + cc

    def turned_rows(part):
        return slice(*((0, 3 * HD), (0, 128), (128, 3 * HD))[0 if part is None else part + 1])

    def give(i, part=None, side=None):
        cc, yy = places[i]
        rows = slice(0, ROWS) if side is None else slice(side * half, (side + 1) * half)
        heads = jnp.dot(
            xbuf[cc, yy, rows], wbuf[1 - zl, :, lanes(part)], preferred_element_type=F32
        ).astype(BF16)
        at = turned_rows(part)
        pbuf[i, at, rows] = heads.T[: at.stop - at.start]
        dst = qkv.at[block(zl, i), at, rows]
        send(pbuf.at[i, at, rows], dst, to_mate, "mate", i, part, side)

    lane = lax.broadcasted_iota(jnp.int32, (ROWS, 128), 1)
    kpos = lax.broadcasted_iota(jnp.int32, (ROWS, 128), 0)
    mark = lax.broadcasted_iota(jnp.int32, (128 - HD, ROWS), 0)
    qpos = lax.broadcasted_iota(jnp.int32, (128 - HD, ROWS), 1)
    cuts = []

    def image_of(pos):
        return sum((pos >= cut).astype(jnp.int32) for cut in cuts)

    def lay_out(b, keys, turned):
        rows = pl.ds(pl.multiple_of(b * ROWS, ROWS), ROWS)
        other = image_of(kpos + b * ROWS) != lane - HD
        kaug[rows, :] = jnp.where(
            lane < HD, keys, jnp.where(other, 1.0, 0.0).astype(BF16)
        )
        own = image_of(qpos + b * ROWS) == mark
        qaug[0:HD, rows] = turned[0:HD]
        qaug[HD:128, rows] = jnp.where(own, -1e30, 0.0).astype(BF16)
        vt[0:48, rows] = turned[80:128]
        vt[48:80, rows] = turned[208:240]

    def take(i):
        cc, yy = places[i]
        heads = jnp.dot(
            xbuf[cc, yy], wbuf[zl], preferred_element_type=F32
        ).astype(BF16)
        lay_out(block(zl, i), heads[:, 128:256], heads.T)

    def receive(i):
        b = block(1 - zl, i)
        if i < 2:
            for part in (0, 1):
                arrived(qkv.at[b, turned_rows(part)], "mate", i, part, None)
        elif i < 6:
            arrived(qkv.at[b, turned_rows(None)], "mate", i, None, None)
        else:
            for side in (0, 1):
                rows = slice(side * half, (side + 1) * half)
                arrived(qkv.at[b, turned_rows(None), rows], "mate", i, None, side)
        turned = qkv[b]
        lay_out(b, turned[128:256].T, turned)

    def quarter(yy, k):
        return xbuf.at[c, yy, pl.ds(k * (half // 2), half // 2), :]

    def pass_on(side):
        arrived(xpart(c, ym, side), "y+", side)
        send(quarter(ym, 2 * side), quarter(ym, 2 * side), to_y[0], "y2", 2 * side)
        arrived(xpart(c, yp, side), "y-", side)
        k = 2 * side + 1
        send(quarter(yp, k), quarter(yp, k), to_y[1], "y2", k)

    loads[2].wait()
    w_here(theirs, 0)
    give(0, 0)
    arrived(xbuf.at[co, y], "c", 0)
    give(1, 0)

    for d in range(1, 8):
        arrived(zbuf.at[behind(d)], "oz", d)
    own_o.wait()
    for zz in range(8):
        lane0 = (zz % 2) * 4 * HD + (zz // 2) * HD
        pack[:, lane0 : lane0 + HD] = zbuf[zz][:, :HD]
    for to, k in zip(to_y, range(3)):
        send(pack, wo_ref.at[c, x, y], to, "oy", k)
    own_pack = keep(pack, wo_ref.at[c, x, y])

    pass_on(0)
    w_here(theirs, 1)
    give(0, 1)
    give(1, 1)
    pass_on(1)
    send(xbuf.at[c, ym], xbuf.at[c, ym], to_co, "c", 1)
    send(xbuf.at[c, yp], xbuf.at[c, yp], to_co, "c", 2)
    give(2)
    give(3)
    arrived(xbuf.at[co, ym], "c", 1)
    give(4)
    arrived(xbuf.at[co, yp], "c", 2)
    give(5)

    loads[3].wait()
    for a in (1, 2, 3):
        count = jnp.sum((ids[...] < a).astype(F32))
        cuts.append(count.astype(jnp.int32))
        cut_ref[a - 1 : a, :] = jnp.full((1, 128), count, F32)
    cut_ref[3:8, :] = jnp.zeros((5, 128), F32)
    kaug[SEQ : SEQ + CK, :] = jnp.ones((CK, 128), BF16)
    vt[:, SEQ : SEQ + CK] = jnp.zeros((HD, CK), BF16)
    own_w.wait()
    w_here((0, *ours), None)
    take(0)
    take(1)

    own_pack.wait()
    for k, yy in enumerate((y, ym, yp, y2)):
        here = wo_ref.at[c, x, yy]
        if k:
            arrived(here, "oy", k - 1)
        send(here, here, to_x[0], "ox", k, 0)
        send(here, here, to_x[1], "ox", k, 1)
    send(wo_ref.at[c, x], wo_ref.at[c, x], to_co, "oc", 0)
    for i in (2, 3, 4, 5):
        take(i)

    for side in (0, 1):
        arrived(quarter(y2, 2 * side), "y2", 2 * side)
        arrived(quarter(y2, 2 * side + 1), "y2", 2 * side + 1)
        send(xpart(c, y2, side), xpart(c, y2, side), to_co, "c", 3 + side)
        give(6, None, side)
        arrived(xpart(co, y2, side), "c", 3 + side)
        give(7, None, side)
    take(6)
    take(7)
    for i in range(5):
        receive(i)

    for k, yy in enumerate((y, ym, yp, y2)):
        arrived(wo_ref.at[c, xm, yy], "ox", k, 0)
        arrived(wo_ref.at[c, xp, yy], "ox", k, 1)
    send(wo_ref.at[c, xm], wo_ref.at[c, xm], to_co, "oc", 1)
    send(wo_ref.at[c, xp], wo_ref.at[c, xp], to_co, "oc", 2)
    for i in (5, 6, 7):
        receive(i)
    for k, xx in enumerate((x, xm, xp)):
        arrived(wo_ref.at[co, xx], "oc", k)
    for cp in sent:
        cp.wait_send()


def in_hbm(a):
    return pltpu.with_memory_space_constraint(a, pltpu.HBM)


def project(patches, ids, w_qkv, w_out):
    return pl.pallas_call(
        project_kernel,
        out_shape=(
            jax.ShapeDtypeStruct((SEQ + CK, 128), BF16),
            jax.ShapeDtypeStruct((128, SEQ), BF16),
            jax.ShapeDtypeStruct((HD, SEQ + CK), BF16),
            jax.ShapeDtypeStruct((8, 128), F32),
            jax.ShapeDtypeStruct((2, 4, 4, HD, 8 * HD), BF16),
        ),
        in_specs=[pl.BlockSpec(memory_space=pltpu.HBM)] * 4,
        out_specs=(pl.BlockSpec(memory_space=pltpu.VMEM),) * 4
        + (pl.BlockSpec(memory_space=pl.ANY),),
        scratch_shapes=[
            pltpu.VMEM((SEQ // 128, 128), jnp.int32),
            pltpu.VMEM((3, HD, HD), BF16),
            pltpu.VMEM((HD, HD), BF16),
            pltpu.VMEM((HD, PACK + 128), BF16),
            pltpu.VMEM((2, 4, ROWS, D), BF16),
            pltpu.VMEM((2, D, PACK), BF16),
            pltpu.VMEM((8, ROWS, PACK), BF16),
            pltpu.VMEM((16, ROWS, PACK), BF16),
            pltpu.VMEM((8, HD, 128), BF16),
            pltpu.VMEM((HD, 8 * HD), BF16),
            pltpu.SemaphoreType.DMA((100,)),
            pltpu.SemaphoreType.DMA((100,)),
            pltpu.SemaphoreType.DMA((8,)),
        ],
        compiler_params=pltpu.CompilerParams(
            collective_id=0, has_side_effects=True, vmem_limit_bytes=40 << 20
        ),
        name="project",
    )(*(in_hbm(a) for a in (patches, ids, w_qkv, w_out)))


def rows_fold(op, a):
    parts = [a[i : i + 8] for i in range(0, a.shape[0], 8)]
    while len(parts) > 1:
        odd = parts[len(parts) // 2 * 2 :]
        parts = [op(l, r) for l, r in zip(parts[::2], parts[1::2])] + odd
    return parts[0]


def attend_kernel(
    cut_ref, kaug, qaug, vt, o_ref, s0, s1, e0, e1, acc, state
):
    cuts = [jnp.max(cut_ref[a : a + 1, :]).astype(jnp.int32) for a in range(3)]
    for ref in (s0, s1, e0, e1, acc, state):
        ref[...] = jnp.zeros_like(ref)

    def span(i):
        first = i * TQ
        lo, hi = jnp.int32(0), jnp.int32(SEQ)
        for cut in cuts:
            lo = jnp.maximum(lo, jnp.where(cut <= first, cut, 0))
            hi = jnp.minimum(hi, jnp.where(cut >= first + TQ, cut, SEQ))
        lo = lax.div(lo, 128) * 128
        return lo, lax.div(hi - lo + CK - 1, CK)

    steps = lax.fori_loop(0, BLOCKS, lambda i, n: n + span(i)[1], jnp.int32(0))

    def step(s_new, s_old, e_old, e_new, carry):
        i1, k1, i2, k2, i3, k3, first2, first3 = carry
        high, top = state[0:1, :], state[8:9, :]
        rescale3, total = state[16:17, :], state[24:32, :]
        before = jnp.where(first2 > 0, -jnp.inf, top)
        top = jnp.maximum(before, high)
        rescale2 = jnp.exp2((before - top) * SCALE)
        block1 = jnp.minimum(i1, BLOCKS - 1)
        query = qaug[:, pl.ds(pl.multiple_of(block1 * TQ, TQ), TQ)]
        highs, sums = [], []
        for u in range(0, CK, SUB):
            part = slice(u, u + SUB)
            keys = kaug[pl.ds(pl.multiple_of(k1 + u, 128), SUB), :]
            s = jnp.dot(keys, query, preferred_element_type=F32)
            s_new[part, :] = s
            highs.append(rows_fold(jnp.maximum, s))
            e = jnp.exp2((s_old[part, :] - top) * SCALE)
            sums.append(rows_fold(jnp.add, e))
            e_new[part, :] = e.astype(BF16)
            if u == 0:
                values = vt[:, pl.ds(pl.multiple_of(k3, 128), CK)]
                mixed = jnp.dot(values, e_old[...], preferred_element_type=F32)
        mixed = acc[...] * rescale3 + mixed
        acc[...] = mixed
        inverse = 1.0 / jnp.sum(total, axis=0, keepdims=True)
        out = pl.ds(pl.multiple_of(i3 * TQ, TQ), TQ)
        o_ref[:, out] = (mixed * inverse).astype(BF16)
        state[0:1, :] = jnp.max(
            functools.reduce(jnp.maximum, highs), axis=0, keepdims=True
        )
        state[8:9, :] = top
        state[16:17, :] = rescale2
        state[24:32, :] = total * rescale2 + functools.reduce(jnp.add, sums)
        lo, n = span(block1)
        first1 = jnp.where(k1 == lo, 1, 0)
        last1 = jnp.where(k1 + CK >= lo + n * CK, 1, 0)
        following = jnp.minimum(i1 + last1, BLOCKS)
        start = span(jnp.minimum(following, BLOCKS - 1))[0]
        k_next = jnp.where(last1 > 0, start, k1 + CK)
        return following, k_next, i1, k1, i2, k2, first1, first2

    def pair(_, carry):
        carry = step(s0, s1, e0, e1, carry)
        return step(s1, s0, e1, e0, carry)

    lax.fori_loop(0, lax.div(steps + 3, 2), pair, (jnp.int32(0),) * 8)


def attend(cuts, kaug, qaug, vt):
    return pl.pallas_call(
        attend_kernel,
        out_shape=jax.ShapeDtypeStruct((HD, SEQ + TQ), BF16),
        in_specs=[pl.BlockSpec(memory_space=pltpu.VMEM)] * 4,
        out_specs=pl.BlockSpec(memory_space=pltpu.VMEM),
        scratch_shapes=[
            pltpu.VMEM((CK, TQ), F32),
            pltpu.VMEM((CK, TQ), F32),
            pltpu.VMEM((CK, TQ), BF16),
            pltpu.VMEM((CK, TQ), BF16),
            pltpu.VMEM((HD, TQ), F32),
            pltpu.VMEM((32, TQ), F32),
        ],
        compiler_params=pltpu.CompilerParams(vmem_limit_bytes=40 << 20),
        name="attend",
    )(cuts, kaug, qaug, vt)


def output_kernel(
    o_ref, wg_ref, out_ref, held, whole, far, total, ssem, rsem, fsend, frecv
):
    x, y, z, c = place()
    dp, me = lax.axis_index("dp"), lax.axis_index("seq")
    zl, co = lax.rem(z, 2), 1 - c
    sides = lax.rem(x + 3, 4), lax.rem(x + 1, 4)
    to_x = device(sides[1], y, z, c), device(sides[0], y, z, c)
    to_co = device(x, y, z, co)
    offsets = [(dz, k) for dz in (0, 1) for k in range(8)][1:]

    def peer(dz, k, back=False):
        plane = lax.rem(zl + dz, 2) * 8
        return plane + lax.rem(lax.rem(me, 8) + (8 - k if back else k), 8)

    barrier = pltpu.get_barrier_semaphore()
    for to in (*((dp, peer(*o)) for o in offsets), *to_x):
        pl.semaphore_signal(barrier, inc=1, device_id=to, device_id_type=MESH)
    pl.semaphore_wait(barrier, 17)

    def cols(s):
        return o_ref.at[:, pl.ds(pl.multiple_of(s * ROWS, ROWS), ROWS)]

    def slot(s):
        return held.at[pl.ds(pl.multiple_of(s * HD, 16), HD), :]

    def copy(src, dst, sems, to):
        return pltpu.make_async_remote_copy(
            src_ref=src,
            dst_ref=dst,
            send_sem=sems[0],
            recv_sem=sems[1],
            device_id=to,
            device_id_type=MESH,
        )

    copies = []
    for n, o in enumerate(offsets):
        to = peer(*o)
        copies.append(copy(cols(to), slot(me), (ssem.at[n], rsem.at[n]), (dp, to)))
        copies[-1].start()
    for yy in range(4):
        side = yy % 2
        copies.append(
            copy(
                wg_ref.at[c, sides[side], yy],
                far.at[c, yy],
                (fsend.at[yy], frecv.at[yy]),
                to_x[side],
            )
        )
        copies[-1].start()
    own = pltpu.make_async_copy(cols(me), slot(me), ssem.at[15])
    own.start()

    def unpack(xx, src):
        @pl.loop(0, 8)
        def _(i):
            block = src[lax.rem(i, 2), lax.div(i, 2)]
            for plane, zh in itertools.product(range(2), range(4)):
                row = pl.multiple_of((plane * 8 + i) * HD, 16)
                col, lane = (zh * 4 + xx) * HD, (plane * 4 + zh) * HD
                whole[pl.ds(row, HD), col : col + HD] = block[:, lane : lane + HD]

    x2 = lax.rem(x + 2, 4)
    for xx in range(4):
        pl.when(xx != x2)(functools.partial(unpack, xx, wg_ref.at[:, xx]))
    for yy in range(4):
        copy(far.at[c, yy], far.at[c, yy], (fsend.at[yy], frecv.at[yy]), to_co).wait_recv()
    copies.append(copy(far.at[c], far.at[c], (fsend.at[4], frecv.at[4]), to_co))
    copies[-1].start()
    copy(far.at[co], far.at[co], (fsend.at[4], frecv.at[4]), to_co).wait_recv()
    for xx in range(4):
        pl.when(xx == x2)(functools.partial(unpack, xx, far))

    def heads(plane):
        rows = pl.ds(pl.multiple_of(plane * 8 * HD, 128), 8 * HD)
        return lax.dot_general(
            held[rows, :],
            whole[rows, :],
            (((0,), (0,)), ((), ())),
            preferred_element_type=F32,
        )

    own.wait()
    for n, o in enumerate(offsets):
        if o[0] == 1 and o[1] == 0:
            total[...] = heads(zl)
        frm = slot(peer(*o, back=True))
        copy(frm, frm, (ssem.at[n], rsem.at[n]), to_co).wait_recv()
    out_ref[...] = (total[...] + heads(1 - zl)).astype(BF16)
    for cp in copies:
        cp.wait_send()


def output(o, wg):
    return pl.pallas_call(
        output_kernel,
        out_shape=jax.ShapeDtypeStruct((ROWS, D), BF16),
        in_specs=[pl.BlockSpec(memory_space=pltpu.VMEM)] * 2,
        out_specs=pl.BlockSpec(memory_space=pltpu.VMEM),
        scratch_shapes=[
            pltpu.VMEM((D, ROWS), BF16),
            pltpu.VMEM((D, D), BF16),
            pltpu.VMEM((2, 4, HD, 8 * HD), BF16),
            pltpu.VMEM((ROWS, D), F32),
            pltpu.SemaphoreType.DMA((16,)),
            pltpu.SemaphoreType.DMA((16,)),
            pltpu.SemaphoreType.DMA((5,)),
            pltpu.SemaphoreType.DMA((5,)),
        ],
        compiler_params=pltpu.CompilerParams(
            collective_id=1, has_side_effects=True, vmem_limit_bytes=40 << 20
        ),
        name="output",
    )(o, wg)


def shards(patches, image_ids, w_qkv, w_out):
    ids = image_ids.reshape(SEQ // 128, 128)
    kaug, qaug, vt, cuts, wo = project(patches[0], ids, w_qkv, w_out)
    o = attend(cuts, kaug, qaug, vt)
    out = output(o, wo)
    return out[None]


def solution(mesh):
    return jax.shard_map(
        shards,
        mesh=mesh,
        in_specs=(P("dp", "seq", None), P("dp", None), P(None, "dp", "seq"), P("seq", "dp")),
        out_specs=P("dp", "seq", None),
        check_vma=False,
    )
```

```python
import functools
import itertools
import math

import jax
import jax.numpy as jnp
from jax import lax
from jax.experimental import pallas as pl
from jax.experimental.pallas import tpu as pltpu
from jax.sharding import PartitionSpec as P

MESH = pl.DeviceIdType.MESH
HD = 80
D = 1280
ROWS = 256
SEQ = 4096
PACK = 256
TQ = 256
CK = 768
SUB = 128
BLOCKS = SEQ // TQ
SCALE = math.log2(math.e) / math.sqrt(HD)
BF16 = jnp.bfloat16
F32 = jnp.float32


def place():
    dp, sq = lax.axis_index("dp"), lax.axis_index("seq")
    x = lax.rem(dp, 4)
    y = lax.rem(lax.div(sq, 2), 4)
    z = lax.div(dp, 4) * 2 + lax.div(sq, 8)
    return x, y, z, lax.rem(sq, 2)


def device(x, y, z, c):
    return (lax.div(z, 2) * 4 + x, lax.rem(z, 2) * 8 + y * 2 + c)


def project_kernel(
    x_ref, ids_ref, wqkv_ref, wout_ref,
    kaug, qaug, vt, cut_ref, wo_ref,
    ids, wq, wo, mine, xbuf, wbuf, pbuf, qkv, zbuf, pack, ssem, rsem, lsem,
):
    x, y, z, c = place()
    zl = lax.rem(z, 2)
    xp, xm, x2 = lax.rem(x + 1, 4), lax.rem(x + 3, 4), lax.rem(x + 2, 4)
    yp, ym, y2 = lax.rem(y + 1, 4), lax.rem(y + 3, 4), lax.rem(y + 2, 4)
    co = 1 - c
    mate = z + 1 - 2 * zl
    to_x = [device(xx, y, z, c) for xx in (xp, xm, x2)]
    to_y = [device(x, yy, z, c) for yy in (yp, ym, y2)]
    to_z = {d: device(x, y, lax.rem(z + d, 8), c) for d in range(1, 8)}
    to_co, to_mate = device(x, y, z, co), device(x, y, mate, c)

    barrier = pltpu.get_barrier_semaphore()
    for to in (*to_x, *to_y, *to_z.values(), to_co):
        pl.semaphore_signal(barrier, inc=1, device_id=to, device_id_type=MESH)

    sent, names, local = [], {}, []

    def sem(*name):
        return names.setdefault(name, len(names))

    def copy(src, dst, k, to):
        return pltpu.make_async_remote_copy(
            src_ref=src,
            dst_ref=dst,
            send_sem=ssem.at[k],
            recv_sem=rsem.at[k],
            device_id=to,
            device_id_type=MESH,
        )

    def send(src, dst, to, *name):
        cp = copy(src, dst, sem(*name), to)
        cp.start()
        sent.append(cp)

    def arrived(dst, *name):
        copy(dst, dst, sem(*name), to_co).wait_recv()

    def keep(src, dst):
        cp = pltpu.make_async_copy(src, dst, lsem.at[len(local)])
        cp.start()
        local.append(cp)
        return cp

    loads = (
        keep(wqkv_ref, wq), keep(wout_ref, wo), keep(x_ref, xbuf.at[c, y]),
        keep(ids_ref, ids),
    )
    loads[0].wait()
    loads[1].wait()
    mine[:, 0:80] = wq[0]
    mine[:, 80:128] = wq[2][:, :48]
    mine[:, 128:208] = wq[1]
    mine[:, 208:240] = wq[2][:, 48:]
    mine[:, 240:256] = jnp.zeros((HD, 16), BF16)
    mine[:, 256:336] = wo[...]
    pl.semaphore_wait(barrier, 14)

    def behind(d):
        return lax.rem(z + 8 - d, 8)

    def lanes(part):
        return slice(0, PACK) if part is None else slice(part * 128, part * 128 + 128)

    def wslot(zz, xx, part=None):
        row = pl.multiple_of((lax.div(zz, 2) * 4 + xx) * HD, 16)
        return wbuf.at[lax.rem(zz, 2), pl.ds(row, HD), lanes(part)]

    half = ROWS // 2

    def xpart(cc, yy, part):
        return xbuf.at[cc, yy, pl.ds(part * half, half), :]

    theirs, ours = (1, 7, 3, 5), (2, 6, 4)
    wo_mine = mine.at[:, PACK : PACK + 128]

    def w_mine(part=None):
        return mine.at[:, lanes(part)]

    for part in (0, 1):
        for d in theirs:
            send(w_mine(part), wslot(z, x, part), to_z[d], "wz", d, part)
    for part in (0, 1):
        src = x_ref.at[pl.ds(part * half, half), :]
        send(src, xpart(c, y, part), to_y[0], "y+", part)
        send(src, xpart(c, y, part), to_y[1], "y-", part)
    send(x_ref, xbuf.at[c, y], to_co, "c", 0)
    for d in ours:
        send(w_mine(), wslot(z, x), to_z[d], "wz", d, None)
    for d in (1, 7, 2, 6, 3, 5, 4):
        send(wo_mine, zbuf.at[z], to_z[d], "oz", d)
    own_w = keep(w_mine(), wslot(z, x))
    own_o = keep(wo_mine, zbuf.at[z])

    def along_x(src, d, part):
        for to, k in zip(to_x, range(3)):
            send(src, wslot(behind(d), x, part), to, "wx", d, part, k)

    for part in (0, 1):
        for d in theirs:
            here = wslot(behind(d), x, part)
            arrived(here, "wz", d, part)
            along_x(here, d, part)
    along_x(w_mine(), 0, None)
    for d in ours:
        here = wslot(behind(d), x)
        arrived(here, "wz", d, None)
        along_x(here, d, None)

    def w_here(ds, part):
        for d in ds:
            for k, xx in enumerate((xm, xp, x2)):
                arrived(wslot(behind(d), xx, part), "wx", d, part, k)

    places = ((c, y), (co, y), (c, ym), (c, yp), (co, ym), (co, yp), (c, y2), (co, y2))

    def block(lo, i):
        cc, yy = places[i]
        return lo * 8 + yy * 2 + cc

    def turned_rows(part):
        return slice(*((0, 3 * HD), (0, 128), (128, 3 * HD))[0 if part is None else part + 1])

    def give(i, part=None, side=None):
        cc, yy = places[i]
        rows = slice(0, ROWS) if side is None else slice(side * half, (side + 1) * half)
        heads = jnp.dot(
            xbuf[cc, yy, rows], wbuf[1 - zl, :, lanes(part)], preferred_element_type=F32
        ).astype(BF16)
        at = turned_rows(part)
        pbuf[i, at, rows] = heads.T[: at.stop - at.start]
        dst = qkv.at[block(zl, i), at, rows]
        send(pbuf.at[i, at, rows], dst, to_mate, "mate", i, part, side)

    lane = lax.broadcasted_iota(jnp.int32, (ROWS, 128), 1)
    kpos = lax.broadcasted_iota(jnp.int32, (ROWS, 128), 0)
    mark = lax.broadcasted_iota(jnp.int32, (128 - HD, ROWS), 0)
    qpos = lax.broadcasted_iota(jnp.int32, (128 - HD, ROWS), 1)
    cuts = []

    def image_of(pos):
        return sum((pos >= cut).astype(jnp.int32) for cut in cuts)

    def lay_out(b, keys, turned):
        rows = pl.ds(pl.multiple_of(b * ROWS, ROWS), ROWS)
        other = image_of(kpos + b * ROWS) != lane - HD
        kaug[rows, :] = jnp.where(
            lane < HD, keys, jnp.where(other, 1.0, 0.0).astype(BF16)
        )
        own = image_of(qpos + b * ROWS) == mark
        qaug[0:HD, rows] = turned[0:HD]
        qaug[HD:128, rows] = jnp.where(own, -1e30, 0.0).astype(BF16)
        vt[0:48, rows] = turned[80:128]
        vt[48:80, rows] = turned[208:240]

    def take(i):
        cc, yy = places[i]
        heads = jnp.dot(
            xbuf[cc, yy], wbuf[zl], preferred_element_type=F32
        ).astype(BF16)
        lay_out(block(zl, i), heads[:, 128:256], heads.T)

    def receive(i):
        b = block(1 - zl, i)
        if i < 2:
            for part in (0, 1):
                arrived(qkv.at[b, turned_rows(part)], "mate", i, part, None)
        elif i < 6:
            arrived(qkv.at[b, turned_rows(None)], "mate", i, None, None)
        else:
            for side in (0, 1):
                rows = slice(side * half, (side + 1) * half)
                arrived(qkv.at[b, turned_rows(None), rows], "mate", i, None, side)
        turned = qkv[b]
        lay_out(b, turned[128:256].T, turned)

    def quarter(yy, k):
        return xbuf.at[c, yy, pl.ds(k * (half // 2), half // 2), :]

    def pass_on(side):
        arrived(xpart(c, ym, side), "y+", side)
        send(quarter(ym, 2 * side), quarter(ym, 2 * side), to_y[0], "y2", 2 * side)
        arrived(xpart(c, yp, side), "y-", side)
        k = 2 * side + 1
        send(quarter(yp, k), quarter(yp, k), to_y[1], "y2", k)

    loads[2].wait()
    w_here(theirs, 0)
    give(0, 0)
    arrived(xbuf.at[co, y], "c", 0)
    give(1, 0)

    for d in range(1, 8):
        arrived(zbuf.at[behind(d)], "oz", d)
    own_o.wait()
    for zz in range(8):
        lane0 = (zz % 2) * 4 * HD + (zz // 2) * HD
        pack[:, lane0 : lane0 + HD] = zbuf[zz][:, :HD]
    for to, k in zip(to_y, range(3)):
        send(pack, wo_ref.at[c, x, y], to, "oy", k)
    own_pack = keep(pack, wo_ref.at[c, x, y])

    pass_on(0)
    w_here(theirs, 1)
    give(0, 1)
    give(1, 1)
    pass_on(1)
    send(xbuf.at[c, ym], xbuf.at[c, ym], to_co, "c", 1)
    send(xbuf.at[c, yp], xbuf.at[c, yp], to_co, "c", 2)
    give(2)
    give(3)
    arrived(xbuf.at[co, ym], "c", 1)
    give(4)
    arrived(xbuf.at[co, yp], "c", 2)
    give(5)

    loads[3].wait()
    for a in (1, 2, 3):
        count = jnp.sum((ids[...] < a).astype(F32))
        cuts.append(count.astype(jnp.int32))
        cut_ref[a - 1 : a, :] = jnp.full((1, 128), count, F32)
    cut_ref[3:8, :] = jnp.zeros((5, 128), F32)
    kaug[SEQ : SEQ + CK, :] = jnp.ones((CK, 128), BF16)
    vt[:, SEQ : SEQ + CK] = jnp.zeros((HD, CK), BF16)
    own_w.wait()
    w_here((0, *ours), None)
    take(0)
    take(1)

    own_pack.wait()
    for k, yy in enumerate((y, ym, yp, y2)):
        here = wo_ref.at[c, x, yy]
        if k:
            arrived(here, "oy", k - 1)
        send(here, here, to_x[0], "ox", k, 0)
        send(here, here, to_x[1], "ox", k, 1)
    send(wo_ref.at[c, x], wo_ref.at[c, x], to_co, "oc", 0)
    for i in (2, 3, 4, 5):
        take(i)

    for side in (0, 1):
        arrived(quarter(y2, 2 * side), "y2", 2 * side)
        arrived(quarter(y2, 2 * side + 1), "y2", 2 * side + 1)
        send(xpart(c, y2, side), xpart(c, y2, side), to_co, "c", 3 + side)
        give(6, None, side)
        arrived(xpart(co, y2, side), "c", 3 + side)
        give(7, None, side)
    take(6)
    take(7)
    for i in range(5):
        receive(i)

    for k, yy in enumerate((y, ym, yp, y2)):
        arrived(wo_ref.at[c, xm, yy], "ox", k, 0)
        arrived(wo_ref.at[c, xp, yy], "ox", k, 1)
    for i in (5, 6, 7):
        receive(i)
    arrived(wo_ref.at[co, x], "oc", 0)
    for cp in sent:
        cp.wait_send()


def in_hbm(a):
    return pltpu.with_memory_space_constraint(a, pltpu.HBM)


def project(patches, ids, w_qkv, w_out):
    return pl.pallas_call(
        project_kernel,
        out_shape=(
            jax.ShapeDtypeStruct((SEQ + CK, 128), BF16),
            jax.ShapeDtypeStruct((128, SEQ), BF16),
            jax.ShapeDtypeStruct((HD, SEQ + CK), BF16),
            jax.ShapeDtypeStruct((8, 128), F32),
            jax.ShapeDtypeStruct((2, 4, 4, HD, 8 * HD), BF16),
        ),
        in_specs=[pl.BlockSpec(memory_space=pltpu.HBM)] * 4,
        out_specs=(pl.BlockSpec(memory_space=pltpu.VMEM),) * 4
        + (pl.BlockSpec(memory_space=pl.ANY),),
        scratch_shapes=[
            pltpu.VMEM((SEQ // 128, 128), jnp.int32),
            pltpu.VMEM((3, HD, HD), BF16),
            pltpu.VMEM((HD, HD), BF16),
            pltpu.VMEM((HD, PACK + 128), BF16),
            pltpu.VMEM((2, 4, ROWS, D), BF16),
            pltpu.VMEM((2, D, PACK), BF16),
            pltpu.VMEM((8, ROWS, PACK), BF16),
            pltpu.VMEM((16, ROWS, PACK), BF16),
            pltpu.VMEM((8, HD, 128), BF16),
            pltpu.VMEM((HD, 8 * HD), BF16),
            pltpu.SemaphoreType.DMA((100,)),
            pltpu.SemaphoreType.DMA((100,)),
            pltpu.SemaphoreType.DMA((8,)),
        ],
        compiler_params=pltpu.CompilerParams(
            collective_id=0, has_side_effects=True, vmem_limit_bytes=40 << 20
        ),
        name="project",
    )(*(in_hbm(a) for a in (patches, ids, w_qkv, w_out)))


def rows_fold(op, a):
    parts = [a[i : i + 8] for i in range(0, a.shape[0], 8)]
    while len(parts) > 1:
        odd = parts[len(parts) // 2 * 2 :]
        parts = [op(l, r) for l, r in zip(parts[::2], parts[1::2])] + odd
    return parts[0]


def attend_kernel(
    cut_ref, kaug, qaug, vt, o_ref, s0, s1, e0, e1, acc, state
):
    cuts = [jnp.max(cut_ref[a : a + 1, :]).astype(jnp.int32) for a in range(3)]
    for ref in (s0, s1, e0, e1, acc, state):
        ref[...] = jnp.zeros_like(ref)

    def span(i):
        first = i * TQ
        lo, hi = jnp.int32(0), jnp.int32(SEQ)
        for cut in cuts:
            lo = jnp.maximum(lo, jnp.where(cut <= first, cut, 0))
            hi = jnp.minimum(hi, jnp.where(cut >= first + TQ, cut, SEQ))
        lo = lax.div(lo, 128) * 128
        return lo, lax.div(hi - lo + CK - 1, CK)

    steps = lax.fori_loop(0, BLOCKS, lambda i, n: n + span(i)[1], jnp.int32(0))

    def step(s_new, s_old, e_old, e_new, carry):
        i1, k1, i2, k2, i3, k3, first2, first3 = carry
        high, top = state[0:1, :], state[8:9, :]
        rescale3, total = state[16:17, :], state[24:32, :]
        before = jnp.where(first2 > 0, -jnp.inf, top)
        top = jnp.maximum(before, high)
        rescale2 = jnp.exp2((before - top) * SCALE)
        block1 = jnp.minimum(i1, BLOCKS - 1)
        query = qaug[:, pl.ds(pl.multiple_of(block1 * TQ, TQ), TQ)]
        highs, sums = [], []
        for u in range(0, CK, SUB):
            part = slice(u, u + SUB)
            keys = kaug[pl.ds(pl.multiple_of(k1 + u, 128), SUB), :]
            s = jnp.dot(keys, query, preferred_element_type=F32)
            s_new[part, :] = s
            highs.append(rows_fold(jnp.maximum, s))
            e = jnp.exp2((s_old[part, :] - top) * SCALE)
            sums.append(rows_fold(jnp.add, e))
            e_new[part, :] = e.astype(BF16)
            if u == 0:
                values = vt[:, pl.ds(pl.multiple_of(k3, 128), CK)]
                mixed = jnp.dot(values, e_old[...], preferred_element_type=F32)
        mixed = acc[...] * rescale3 + mixed
        acc[...] = mixed
        inverse = 1.0 / jnp.sum(total, axis=0, keepdims=True)
        out = pl.ds(pl.multiple_of(i3 * TQ, TQ), TQ)
        o_ref[:, out] = (mixed * inverse).astype(BF16)
        state[0:1, :] = jnp.max(
            functools.reduce(jnp.maximum, highs), axis=0, keepdims=True
        )
        state[8:9, :] = top
        state[16:17, :] = rescale2
        state[24:32, :] = total * rescale2 + functools.reduce(jnp.add, sums)
        lo, n = span(block1)
        first1 = jnp.where(k1 == lo, 1, 0)
        last1 = jnp.where(k1 + CK >= lo + n * CK, 1, 0)
        following = jnp.minimum(i1 + last1, BLOCKS)
        start = span(jnp.minimum(following, BLOCKS - 1))[0]
        k_next = jnp.where(last1 > 0, start, k1 + CK)
        return following, k_next, i1, k1, i2, k2, first1, first2

    def pair(_, carry):
        carry = step(s0, s1, e0, e1, carry)
        return step(s1, s0, e1, e0, carry)

    lax.fori_loop(0, lax.div(steps + 3, 2), pair, (jnp.int32(0),) * 8)


def attend(cuts, kaug, qaug, vt):
    return pl.pallas_call(
        attend_kernel,
        out_shape=jax.ShapeDtypeStruct((HD, SEQ + TQ), BF16),
        in_specs=[pl.BlockSpec(memory_space=pltpu.VMEM)] * 4,
        out_specs=pl.BlockSpec(memory_space=pltpu.VMEM),
        scratch_shapes=[
            pltpu.VMEM((CK, TQ), F32),
            pltpu.VMEM((CK, TQ), F32),
            pltpu.VMEM((CK, TQ), BF16),
            pltpu.VMEM((CK, TQ), BF16),
            pltpu.VMEM((HD, TQ), F32),
            pltpu.VMEM((32, TQ), F32),
        ],
        compiler_params=pltpu.CompilerParams(vmem_limit_bytes=40 << 20),
        name="attend",
    )(cuts, kaug, qaug, vt)


def output_kernel(
    o_ref, wg_ref, out_ref, held, whole, far, near, total, ssem, rsem, fsend, frecv
):
    x, y, z, c = place()
    dp, me = lax.axis_index("dp"), lax.axis_index("seq")
    zl, co = lax.rem(z, 2), 1 - c
    sides = lax.rem(x + 3, 4), lax.rem(x + 1, 4)
    to_x = device(sides[1], y, z, c), device(sides[0], y, z, c)
    to_co = device(x, y, z, co)
    offsets = [(dz, k) for dz in (1, 0) for k in range(8) if dz or k]

    def peer(dz, k, back=False):
        plane = lax.rem(zl + dz, 2) * 8
        return plane + lax.rem(lax.rem(me, 8) + (8 - k if back else k), 8)

    barrier = pltpu.get_barrier_semaphore()
    for to in (*((dp, peer(*o)) for o in offsets), *to_x):
        pl.semaphore_signal(barrier, inc=1, device_id=to, device_id_type=MESH)
    pl.semaphore_wait(barrier, 17)

    def cols(s):
        return o_ref.at[:, pl.ds(pl.multiple_of(s * ROWS, ROWS), ROWS)]

    def slot(s):
        return held.at[pl.ds(pl.multiple_of(s * HD, 16), HD), :]

    def copy(src, dst, sems, to):
        return pltpu.make_async_remote_copy(
            src_ref=src,
            dst_ref=dst,
            send_sem=sems[0],
            recv_sem=sems[1],
            device_id=to,
            device_id_type=MESH,
        )

    copies = []
    for yy in range(4):
        side = yy % 2
        copies.append(
            copy(
                wg_ref.at[c, sides[side], yy],
                far.at[c, yy],
                (fsend.at[yy], frecv.at[yy]),
                to_x[side],
            )
        )
        copies[-1].start()
    for n, o in enumerate(offsets):
        to = peer(*o)
        copies.append(copy(cols(to), slot(me), (ssem.at[n], rsem.at[n]), (dp, to)))
        copies[-1].start()
    crossing = []
    for side in (0, 1):
        sems = fsend.at[5 + side], frecv.at[5 + side]
        copies.append(copy(wg_ref.at[c, sides[side]], near.at[side], sems, to_co))
        copies[-1].start()
        crossing.append(copy(near.at[side], near.at[side], sems, to_co))
    own = pltpu.make_async_copy(cols(me), slot(me), ssem.at[15])
    own.start()

    def unpack(xx, ours, others):
        @pl.loop(0, 4)
        def _(yy):
            for core, src in ((c, ours), (co, others)):
                block = src[yy]
                for plane, zh in itertools.product(range(2), range(4)):
                    row = pl.multiple_of((plane * 8 + yy * 2 + core) * HD, 16)
                    col, lane = (zh * 4 + xx) * HD, (plane * 4 + zh) * HD
                    whole[pl.ds(row, HD), col : col + HD] = block[:, lane : lane + HD]

    def unpack_if(where, ours, others):
        for xx in range(4):
            pl.when(xx == where)(functools.partial(unpack, xx, ours, others))

    unpack_if(x, wg_ref.at[c, x], wg_ref.at[co, x])
    for side in (0, 1):
        crossing[side].wait_recv()
        unpack_if(sides[side], wg_ref.at[c, sides[side]], near.at[side])
    for yy in range(4):
        copy(far.at[c, yy], far.at[c, yy], (fsend.at[yy], frecv.at[yy]), to_co).wait_recv()
    copies.append(copy(far.at[c], far.at[c], (fsend.at[4], frecv.at[4]), to_co))
    copies[-1].start()
    copy(far.at[co], far.at[co], (fsend.at[4], frecv.at[4]), to_co).wait_recv()
    unpack_if(lax.rem(x + 2, 4), far.at[c], far.at[co])

    def heads(plane):
        rows = pl.ds(pl.multiple_of(plane * 8 * HD, 128), 8 * HD)
        return lax.dot_general(
            held[rows, :],
            whole[rows, :],
            (((0,), (0,)), ((), ())),
            preferred_element_type=F32,
        )

    own.wait()
    for n, o in enumerate(offsets):
        if o == (0, 1):
            total[...] = heads(1 - zl)
        frm = slot(peer(*o, back=True))
        copy(frm, frm, (ssem.at[n], rsem.at[n]), to_co).wait_recv()
    out_ref[...] = (total[...] + heads(zl)).astype(BF16)
    for cp in copies:
        cp.wait_send()


def output(o, wg):
    return pl.pallas_call(
        output_kernel,
        out_shape=jax.ShapeDtypeStruct((ROWS, D), BF16),
        in_specs=[pl.BlockSpec(memory_space=pltpu.VMEM)] * 2,
        out_specs=pl.BlockSpec(memory_space=pltpu.VMEM),
        scratch_shapes=[
            pltpu.VMEM((D, ROWS), BF16),
            pltpu.VMEM((D, D), BF16),
            pltpu.VMEM((2, 4, HD, 8 * HD), BF16),
            pltpu.VMEM((2, 4, HD, 8 * HD), BF16),
            pltpu.VMEM((ROWS, D), F32),
            pltpu.SemaphoreType.DMA((16,)),
            pltpu.SemaphoreType.DMA((16,)),
            pltpu.SemaphoreType.DMA((7,)),
            pltpu.SemaphoreType.DMA((7,)),
        ],
        compiler_params=pltpu.CompilerParams(
            collective_id=1, has_side_effects=True, vmem_limit_bytes=40 << 20
        ),
        name="output",
    )(o, wg)


def shards(patches, image_ids, w_qkv, w_out):
    ids = image_ids.reshape(SEQ // 128, 128)
    kaug, qaug, vt, cuts, wo = project(patches[0], ids, w_qkv, w_out)
    o = attend(cuts, kaug, qaug, vt)
    out = output(o, wo)
    return out[None]


def solution(mesh):
    return jax.shard_map(
        shards,
        mesh=mesh,
        in_specs=(P("dp", "seq", None), P("dp", None), P(None, "dp", "seq"), P("seq", "dp")),
        out_specs=P("dp", "seq", None),
        check_vma=False,
    )
```

```python
import functools
import itertools
import math

import jax
import jax.numpy as jnp
from jax import lax
from jax.experimental import pallas as pl
from jax.experimental.pallas import tpu as pltpu
from jax.sharding import PartitionSpec as P

MESH = pl.DeviceIdType.MESH
HD = 80
D = 1280
ROWS = 256
SEQ = 4096
PACK = 256
TQ = 256
CK = 768
SUB = 128
BLOCKS = SEQ // TQ
SCALE = math.log2(math.e) / math.sqrt(HD)
BF16 = jnp.bfloat16
F32 = jnp.float32


def place():
    dp, sq = lax.axis_index("dp"), lax.axis_index("seq")
    x = lax.rem(dp, 4)
    y = lax.rem(lax.div(sq, 2), 4)
    z = lax.div(dp, 4) * 2 + lax.div(sq, 8)
    return x, y, z, lax.rem(sq, 2)


def device(x, y, z, c):
    return (lax.div(z, 2) * 4 + x, lax.rem(z, 2) * 8 + y * 2 + c)


def project_kernel(
    x_ref, ids_ref, wqkv_ref, wout_ref,
    kaug, qaug, vt, cut_ref, wo_ref,
    ids, wq, wo, mine, xbuf, wbuf, pbuf, qkv, zbuf, pack, ssem, rsem, lsem,
):
    x, y, z, c = place()
    zl = lax.rem(z, 2)
    xp, xm, x2 = lax.rem(x + 1, 4), lax.rem(x + 3, 4), lax.rem(x + 2, 4)
    yp, ym, y2 = lax.rem(y + 1, 4), lax.rem(y + 3, 4), lax.rem(y + 2, 4)
    co = 1 - c
    mate = z + 1 - 2 * zl
    to_x = [device(xx, y, z, c) for xx in (xp, xm, x2)]
    to_y = [device(x, yy, z, c) for yy in (yp, ym, y2)]
    to_z = {d: device(x, y, lax.rem(z + d, 8), c) for d in range(1, 8)}
    to_co, to_mate = device(x, y, z, co), device(x, y, mate, c)

    barrier = pltpu.get_barrier_semaphore()
    for to in (*to_x, *to_y, *to_z.values(), to_co):
        pl.semaphore_signal(barrier, inc=1, device_id=to, device_id_type=MESH)

    sent, names, local = [], {}, []

    def sem(*name):
        return names.setdefault(name, len(names))

    def copy(src, dst, k, to):
        return pltpu.make_async_remote_copy(
            src_ref=src,
            dst_ref=dst,
            send_sem=ssem.at[k],
            recv_sem=rsem.at[k],
            device_id=to,
            device_id_type=MESH,
        )

    def send(src, dst, to, *name):
        cp = copy(src, dst, sem(*name), to)
        cp.start()
        sent.append(cp)

    def arrived(dst, *name):
        copy(dst, dst, sem(*name), to_co).wait_recv()

    def keep(src, dst):
        cp = pltpu.make_async_copy(src, dst, lsem.at[len(local)])
        cp.start()
        local.append(cp)
        return cp

    loads = (
        keep(wqkv_ref, wq), keep(wout_ref, wo), keep(x_ref, xbuf.at[c, y]),
        keep(ids_ref, ids),
    )
    loads[0].wait()
    loads[1].wait()
    mine[:, 0:80] = wq[0]
    mine[:, 80:128] = wq[2][:, :48]
    mine[:, 128:208] = wq[1]
    mine[:, 208:240] = wq[2][:, 48:]
    mine[:, 240:256] = jnp.zeros((HD, 16), BF16)
    mine[:, 256:336] = wo[...]
    pl.semaphore_wait(barrier, 14)

    def behind(d):
        return lax.rem(z + 8 - d, 8)

    def lanes(part):
        return slice(0, PACK) if part is None else slice(part * 128, part * 128 + 128)

    def wslot(zz, xx, part=None):
        row = pl.multiple_of((lax.div(zz, 2) * 4 + xx) * HD, 16)
        return wbuf.at[lax.rem(zz, 2), pl.ds(row, HD), lanes(part)]

    half = ROWS // 2

    def xpart(cc, yy, part):
        return xbuf.at[cc, yy, pl.ds(part * half, half), :]

    theirs, ours = (1, 7, 3, 5), (2, 6, 4)
    wo_mine = mine.at[:, PACK : PACK + 128]

    def w_mine(part=None):
        return mine.at[:, lanes(part)]

    for part in (0, 1):
        for d in theirs:
            send(w_mine(part), wslot(z, x, part), to_z[d], "wz", d, part)
    for part in (0, 1):
        src = x_ref.at[pl.ds(part * half, half), :]
        send(src, xpart(c, y, part), to_y[0], "y+", part)
        send(src, xpart(c, y, part), to_y[1], "y-", part)
    send(x_ref, xbuf.at[c, y], to_co, "c", 0)
    for d in ours:
        send(w_mine(), wslot(z, x), to_z[d], "wz", d, None)
    for d in (1, 7, 2, 6, 3, 5, 4):
        send(wo_mine, zbuf.at[z], to_z[d], "oz", d)
    own_w = keep(w_mine(), wslot(z, x))
    own_o = keep(wo_mine, zbuf.at[z])

    def along_x(src, d, part):
        for to, k in zip(to_x, range(3)):
            send(src, wslot(behind(d), x, part), to, "wx", d, part, k)

    for part in (0, 1):
        for d in theirs:
            here = wslot(behind(d), x, part)
            arrived(here, "wz", d, part)
            along_x(here, d, part)
    along_x(w_mine(), 0, None)
    for d in ours:
        here = wslot(behind(d), x)
        arrived(here, "wz", d, None)
        along_x(here, d, None)

    def w_here(ds, part):
        for d in ds:
            for k, xx in enumerate((xm, xp, x2)):
                arrived(wslot(behind(d), xx, part), "wx", d, part, k)

    places = ((c, y), (co, y), (c, ym), (c, yp), (co, ym), (co, yp), (c, y2), (co, y2))

    def block(lo, i):
        cc, yy = places[i]
        return lo * 8 + yy * 2 + cc

    def turned_rows(part):
        return slice(*((0, 3 * HD), (0, 128), (128, 3 * HD))[0 if part is None else part + 1])

    def give(i, part=None, side=None):
        cc, yy = places[i]
        rows = slice(0, ROWS) if side is None else slice(side * half, (side + 1) * half)
        heads = jnp.dot(
            xbuf[cc, yy, rows], wbuf[1 - zl, :, lanes(part)], preferred_element_type=F32
        ).astype(BF16)
        at = turned_rows(part)
        pbuf[i, at, rows] = heads.T[: at.stop - at.start]
        dst = qkv.at[block(zl, i), at, rows]
        send(pbuf.at[i, at, rows], dst, to_mate, "mate", i, part, side)

    lane = lax.broadcasted_iota(jnp.int32, (ROWS, 128), 1)
    kpos = lax.broadcasted_iota(jnp.int32, (ROWS, 128), 0)
    mark = lax.broadcasted_iota(jnp.int32, (128 - HD, ROWS), 0)
    qpos = lax.broadcasted_iota(jnp.int32, (128 - HD, ROWS), 1)
    cuts = []

    def image_of(pos):
        return sum((pos >= cut).astype(jnp.int32) for cut in cuts)

    def lay_out(b, keys, turned):
        rows = pl.ds(pl.multiple_of(b * ROWS, ROWS), ROWS)
        other = image_of(kpos + b * ROWS) != lane - HD
        kaug[rows, :] = jnp.where(
            lane < HD, keys, jnp.where(other, 1.0, 0.0).astype(BF16)
        )
        own = image_of(qpos + b * ROWS) == mark
        qaug[0:HD, rows] = turned[0:HD]
        qaug[HD:128, rows] = jnp.where(own, -1e30, 0.0).astype(BF16)
        vt[0:48, rows] = turned[80:128]
        vt[48:80, rows] = turned[208:240]

    def take(i):
        cc, yy = places[i]
        heads = jnp.dot(
            xbuf[cc, yy], wbuf[zl], preferred_element_type=F32
        ).astype(BF16)
        lay_out(block(zl, i), heads[:, 128:256], heads.T)

    def receive(i):
        b = block(1 - zl, i)
        if i < 2:
            for part in (0, 1):
                arrived(qkv.at[b, turned_rows(part)], "mate", i, part, None)
        elif i < 6:
            arrived(qkv.at[b, turned_rows(None)], "mate", i, None, None)
        else:
            for side in (0, 1):
                rows = slice(side * half, (side + 1) * half)
                arrived(qkv.at[b, turned_rows(None), rows], "mate", i, None, side)
        turned = qkv[b]
        lay_out(b, turned[128:256].T, turned)

    def quarter(yy, k):
        return xbuf.at[c, yy, pl.ds(k * (half // 2), half // 2), :]

    def pass_on(side):
        arrived(xpart(c, ym, side), "y+", side)
        send(quarter(ym, 2 * side), quarter(ym, 2 * side), to_y[0], "y2", 2 * side)
        arrived(xpart(c, yp, side), "y-", side)
        k = 2 * side + 1
        send(quarter(yp, k), quarter(yp, k), to_y[1], "y2", k)

    loads[2].wait()
    w_here(theirs, 0)
    give(0, 0)
    arrived(xbuf.at[co, y], "c", 0)
    give(1, 0)

    for d in range(1, 8):
        arrived(zbuf.at[behind(d)], "oz", d)
    own_o.wait()
    for zz in range(8):
        lane0 = (zz % 2) * 4 * HD + (zz // 2) * HD
        pack[:, lane0 : lane0 + HD] = zbuf[zz][:, :HD]
    for to, k in zip(to_y, range(3)):
        send(pack, wo_ref.at[c, x, y], to, "oy", k)
    send(pack, wo_ref.at[c, x, y], to_x[0], "ox", 0, 0)
    send(pack, wo_ref.at[c, x, y], to_x[1], "ox", 0, 1)
    own_pack = keep(pack, wo_ref.at[c, x, y])

    pass_on(0)
    w_here(theirs, 1)
    give(0, 1)
    give(1, 1)
    pass_on(1)
    send(xbuf.at[c, ym], xbuf.at[c, ym], to_co, "c", 1)
    send(xbuf.at[c, yp], xbuf.at[c, yp], to_co, "c", 2)
    give(2)
    give(3)
    arrived(xbuf.at[co, ym], "c", 1)
    give(4)
    arrived(xbuf.at[co, yp], "c", 2)
    give(5)

    loads[3].wait()
    for a in (1, 2, 3):
        count = jnp.sum((ids[...] < a).astype(F32))
        cuts.append(count.astype(jnp.int32))
        cut_ref[a - 1 : a, :] = jnp.full((1, 128), count, F32)
    cut_ref[3:8, :] = jnp.zeros((5, 128), F32)
    kaug[SEQ : SEQ + CK, :] = jnp.ones((CK, 128), BF16)
    vt[:, SEQ : SEQ + CK] = jnp.zeros((HD, CK), BF16)
    own_w.wait()
    w_here((0, *ours), None)
    take(0)
    take(1)

    own_pack.wait()
    for k, yy in enumerate((y, ym, yp, y2)):
        here = wo_ref.at[c, x, yy]
        if not k:
            continue
        arrived(here, "oy", k - 1)
        send(here, here, to_x[0], "ox", k, 0)
        send(here, here, to_x[1], "ox", k, 1)
    send(wo_ref.at[c, x], wo_ref.at[c, x], to_co, "oc", 0)
    for i in (2, 3, 4, 5):
        take(i)

    for side in (0, 1):
        arrived(quarter(y2, 2 * side), "y2", 2 * side)
        arrived(quarter(y2, 2 * side + 1), "y2", 2 * side + 1)
        send(xpart(c, y2, side), xpart(c, y2, side), to_co, "c", 3 + side)
        give(6, None, side)
        arrived(xpart(co, y2, side), "c", 3 + side)
        give(7, None, side)
    take(6)
    take(7)
    for i in range(5):
        receive(i)

    for k, yy in enumerate((y, ym, yp, y2)):
        arrived(wo_ref.at[c, xm, yy], "ox", k, 0)
        arrived(wo_ref.at[c, xp, yy], "ox", k, 1)
    for i in (5, 6, 7):
        receive(i)
    arrived(wo_ref.at[co, x], "oc", 0)
    for cp in sent:
        cp.wait_send()


def in_hbm(a):
    return pltpu.with_memory_space_constraint(a, pltpu.HBM)


def project(patches, ids, w_qkv, w_out):
    return pl.pallas_call(
        project_kernel,
        out_shape=(
            jax.ShapeDtypeStruct((SEQ + CK, 128), BF16),
            jax.ShapeDtypeStruct((128, SEQ), BF16),
            jax.ShapeDtypeStruct((HD, SEQ + CK), BF16),
            jax.ShapeDtypeStruct((8, 128), F32),
            jax.ShapeDtypeStruct((2, 4, 4, HD, 8 * HD), BF16),
        ),
        in_specs=[pl.BlockSpec(memory_space=pltpu.HBM)] * 4,
        out_specs=(pl.BlockSpec(memory_space=pltpu.VMEM),) * 4
        + (pl.BlockSpec(memory_space=pl.ANY),),
        scratch_shapes=[
            pltpu.VMEM((SEQ // 128, 128), jnp.int32),
            pltpu.VMEM((3, HD, HD), BF16),
            pltpu.VMEM((HD, HD), BF16),
            pltpu.VMEM((HD, PACK + 128), BF16),
            pltpu.VMEM((2, 4, ROWS, D), BF16),
            pltpu.VMEM((2, D, PACK), BF16),
            pltpu.VMEM((8, ROWS, PACK), BF16),
            pltpu.VMEM((16, ROWS, PACK), BF16),
            pltpu.VMEM((8, HD, 128), BF16),
            pltpu.VMEM((HD, 8 * HD), BF16),
            pltpu.SemaphoreType.DMA((100,)),
            pltpu.SemaphoreType.DMA((100,)),
            pltpu.SemaphoreType.DMA((8,)),
        ],
        compiler_params=pltpu.CompilerParams(
            collective_id=0, has_side_effects=True, vmem_limit_bytes=40 << 20
        ),
        name="project",
    )(*(in_hbm(a) for a in (patches, ids, w_qkv, w_out)))


def rows_fold(op, a):
    parts = [a[i : i + 8] for i in range(0, a.shape[0], 8)]
    while len(parts) > 1:
        odd = parts[len(parts) // 2 * 2 :]
        parts = [op(l, r) for l, r in zip(parts[::2], parts[1::2])] + odd
    return parts[0]


def attend_kernel(
    cut_ref, kaug, qaug, vt, o_ref, s0, s1, e0, e1, acc, state
):
    cuts = [jnp.max(cut_ref[a : a + 1, :]).astype(jnp.int32) for a in range(3)]
    for ref in (s0, s1, e0, e1, acc, state):
        ref[...] = jnp.zeros_like(ref)

    def span(i):
        first = i * TQ
        lo, hi = jnp.int32(0), jnp.int32(SEQ)
        for cut in cuts:
            lo = jnp.maximum(lo, jnp.where(cut <= first, cut, 0))
            hi = jnp.minimum(hi, jnp.where(cut >= first + TQ, cut, SEQ))
        lo = lax.div(lo, 128) * 128
        return lo, lax.div(hi - lo + CK - 1, CK)

    steps = lax.fori_loop(0, BLOCKS, lambda i, n: n + span(i)[1], jnp.int32(0))

    def step(s_new, s_old, e_old, e_new, carry):
        i1, k1, i2, k2, i3, k3, first2, first3 = carry
        high, top = state[0:1, :], state[8:9, :]
        rescale3, total = state[16:17, :], state[24:32, :]
        before = jnp.where(first2 > 0, -jnp.inf, top)
        top = jnp.maximum(before, high)
        rescale2 = jnp.exp2((before - top) * SCALE)
        block1 = jnp.minimum(i1, BLOCKS - 1)
        query = qaug[:, pl.ds(pl.multiple_of(block1 * TQ, TQ), TQ)]
        highs, sums = [], []
        for u in range(0, CK, SUB):
            part = slice(u, u + SUB)
            keys = kaug[pl.ds(pl.multiple_of(k1 + u, 128), SUB), :]
            s = jnp.dot(keys, query, preferred_element_type=F32)
            s_new[part, :] = s
            highs.append(rows_fold(jnp.maximum, s))
            e = jnp.exp2((s_old[part, :] - top) * SCALE)
            sums.append(rows_fold(jnp.add, e))
            e_new[part, :] = e.astype(BF16)
            if u == 0:
                values = vt[:, pl.ds(pl.multiple_of(k3, 128), CK)]
                mixed = jnp.dot(values, e_old[...], preferred_element_type=F32)
        mixed = acc[...] * rescale3 + mixed
        acc[...] = mixed
        inverse = 1.0 / jnp.sum(total, axis=0, keepdims=True)
        out = pl.ds(pl.multiple_of(i3 * TQ, TQ), TQ)
        o_ref[:, out] = (mixed * inverse).astype(BF16)
        state[0:1, :] = jnp.max(
            functools.reduce(jnp.maximum, highs), axis=0, keepdims=True
        )
        state[8:9, :] = top
        state[16:17, :] = rescale2
        state[24:32, :] = total * rescale2 + functools.reduce(jnp.add, sums)
        lo, n = span(block1)
        first1 = jnp.where(k1 == lo, 1, 0)
        last1 = jnp.where(k1 + CK >= lo + n * CK, 1, 0)
        following = jnp.minimum(i1 + last1, BLOCKS)
        start = span(jnp.minimum(following, BLOCKS - 1))[0]
        k_next = jnp.where(last1 > 0, start, k1 + CK)
        return following, k_next, i1, k1, i2, k2, first1, first2

    def pair(_, carry):
        carry = step(s0, s1, e0, e1, carry)
        return step(s1, s0, e1, e0, carry)

    lax.fori_loop(0, lax.div(steps + 3, 2), pair, (jnp.int32(0),) * 8)


def attend(cuts, kaug, qaug, vt):
    return pl.pallas_call(
        attend_kernel,
        out_shape=jax.ShapeDtypeStruct((HD, SEQ + TQ), BF16),
        in_specs=[pl.BlockSpec(memory_space=pltpu.VMEM)] * 4,
        out_specs=pl.BlockSpec(memory_space=pltpu.VMEM),
        scratch_shapes=[
            pltpu.VMEM((CK, TQ), F32),
            pltpu.VMEM((CK, TQ), F32),
            pltpu.VMEM((CK, TQ), BF16),
            pltpu.VMEM((CK, TQ), BF16),
            pltpu.VMEM((HD, TQ), F32),
            pltpu.VMEM((32, TQ), F32),
        ],
        compiler_params=pltpu.CompilerParams(vmem_limit_bytes=40 << 20),
        name="attend",
    )(cuts, kaug, qaug, vt)


def output_kernel(
    o_ref, wg_ref, out_ref, held, whole, far, near, total, ssem, rsem, fsend, frecv
):
    x, y, z, c = place()
    dp, me = lax.axis_index("dp"), lax.axis_index("seq")
    zl, co = lax.rem(z, 2), 1 - c
    sides = lax.rem(x + 3, 4), lax.rem(x + 1, 4)
    to_x = device(sides[1], y, z, c), device(sides[0], y, z, c)
    to_co = device(x, y, z, co)
    offsets = [(dz, k) for dz in (1, 0) for k in range(8) if dz or k]

    def peer(dz, k, back=False):
        plane = lax.rem(zl + dz, 2) * 8
        return plane + lax.rem(lax.rem(me, 8) + (8 - k if back else k), 8)

    barrier = pltpu.get_barrier_semaphore()
    for to in (*((dp, peer(*o)) for o in offsets), *to_x):
        pl.semaphore_signal(barrier, inc=1, device_id=to, device_id_type=MESH)
    pl.semaphore_wait(barrier, 17)

    def cols(s):
        return o_ref.at[:, pl.ds(pl.multiple_of(s * ROWS, ROWS), ROWS)]

    def slot(s):
        return held.at[pl.ds(pl.multiple_of(s * HD, 16), HD), :]

    def copy(src, dst, sems, to):
        return pltpu.make_async_remote_copy(
            src_ref=src,
            dst_ref=dst,
            send_sem=sems[0],
            recv_sem=sems[1],
            device_id=to,
            device_id_type=MESH,
        )

    copies = []
    for yy in range(4):
        side = yy % 2
        copies.append(
            copy(
                wg_ref.at[c, sides[side], yy],
                far.at[c, yy],
                (fsend.at[yy], frecv.at[yy]),
                to_x[side],
            )
        )
        copies[-1].start()
    for n, o in enumerate(offsets):
        to = peer(*o)
        copies.append(copy(cols(to), slot(me), (ssem.at[n], rsem.at[n]), (dp, to)))
        copies[-1].start()
    crossing = []
    for side in (0, 1):
        sems = fsend.at[5 + side], frecv.at[5 + side]
        copies.append(copy(wg_ref.at[c, sides[side]], near.at[side], sems, to_co))
        copies[-1].start()
        crossing.append(copy(near.at[side], near.at[side], sems, to_co))
    own = pltpu.make_async_copy(cols(me), slot(me), ssem.at[15])
    own.start()

    def unpack(xx, ours, others):
        @pl.loop(0, 4)
        def _(yy):
            for core, src in ((c, ours), (co, others)):
                block = src[yy]
                for plane, zh in itertools.product(range(2), range(4)):
                    row = pl.multiple_of((plane * 8 + yy * 2 + core) * HD, 16)
                    col, lane = (zh * 4 + xx) * HD, (plane * 4 + zh) * HD
                    whole[pl.ds(row, HD), col : col + HD] = block[:, lane : lane + HD]

    def unpack_if(where, ours, others):
        for xx in range(4):
            pl.when(xx == where)(functools.partial(unpack, xx, ours, others))

    unpack_if(x, wg_ref.at[c, x], wg_ref.at[co, x])
    for side in (0, 1):
        crossing[side].wait_recv()
        unpack_if(sides[side], wg_ref.at[c, sides[side]], near.at[side])
    for yy in range(4):
        copy(far.at[c, yy], far.at[c, yy], (fsend.at[yy], frecv.at[yy]), to_co).wait_recv()
    copies.append(copy(far.at[c], far.at[c], (fsend.at[4], frecv.at[4]), to_co))
    copies[-1].start()
    copy(far.at[co], far.at[co], (fsend.at[4], frecv.at[4]), to_co).wait_recv()
    unpack_if(lax.rem(x + 2, 4), far.at[c], far.at[co])

    def heads(plane):
        rows = pl.ds(pl.multiple_of(plane * 8 * HD, 128), 8 * HD)
        return lax.dot_general(
            held[rows, :],
            whole[rows, :],
            (((0,), (0,)), ((), ())),
            preferred_element_type=F32,
        )

    own.wait()
    for n, o in enumerate(offsets):
        if o == (0, 1):
            total[...] = heads(1 - zl)
        frm = slot(peer(*o, back=True))
        copy(frm, frm, (ssem.at[n], rsem.at[n]), to_co).wait_recv()
    out_ref[...] = (total[...] + heads(zl)).astype(BF16)
    for cp in copies:
        cp.wait_send()


def output(o, wg):
    return pl.pallas_call(
        output_kernel,
        out_shape=jax.ShapeDtypeStruct((ROWS, D), BF16),
        in_specs=[pl.BlockSpec(memory_space=pltpu.VMEM)] * 2,
        out_specs=pl.BlockSpec(memory_space=pltpu.VMEM),
        scratch_shapes=[
            pltpu.VMEM((D, ROWS), BF16),
            pltpu.VMEM((D, D), BF16),
            pltpu.VMEM((2, 4, HD, 8 * HD), BF16),
            pltpu.VMEM((2, 4, HD, 8 * HD), BF16),
            pltpu.VMEM((ROWS, D), F32),
            pltpu.SemaphoreType.DMA((16,)),
            pltpu.SemaphoreType.DMA((16,)),
            pltpu.SemaphoreType.DMA((7,)),
            pltpu.SemaphoreType.DMA((7,)),
        ],
        compiler_params=pltpu.CompilerParams(
            collective_id=1, has_side_effects=True, vmem_limit_bytes=40 << 20
        ),
        name="output",
    )(o, wg)


def shards(patches, image_ids, w_qkv, w_out):
    ids = image_ids.reshape(SEQ // 128, 128)
    kaug, qaug, vt, cuts, wo = project(patches[0], ids, w_qkv, w_out)
    o = attend(cuts, kaug, qaug, vt)
    out = output(o, wo)
    return out[None]


def solution(mesh):
    return jax.shard_map(
        shards,
        mesh=mesh,
        in_specs=(P("dp", "seq", None), P("dp", None), P(None, "dp", "seq"), P("seq", "dp")),
        out_specs=P("dp", "seq", None),
        check_vma=False,
    )
```
